256 devices in a mesh: crop: 4 (over y), dap: 64 (over x, z, core).
Axes of the slice: x: 4, y: 4, z: 8, core: 2. Of those that a mesh axis runs over, the one named last changes fastest.
Arguments:
- pair: float32 [768, 192, 128], P(('crop', 'dap')), parts along dimension 0, may hold values from -6 to 6
- norm_in: float32 [2, 128], replicated, may hold values from 0.1 to 1.9
- w_proj: bfloat16 [2, 128, 512], replicated, may hold values from -0.5 to 0.5
- w_gate: bfloat16 [2, 128, 128], replicated, may hold values from -0.5 to 0.5
- norm_mid: float32 [2, 128], replicated, may hold values from 0.1 to 1.9
- w_out: bfloat16 [2, 128, 128], replicated, may hold values from -0.5 to 0.5
Outputs:
- pair_out: float32 [768, 192, 128], P(('crop', 'dap')), parts along dimension 0
The draws below stay inside these ranges and needn't reach their ends.
There are 4 independent parts, one for each index of `crop`. The reference program is written for one: setup_inputs(seed, part) draws one part's arguments, and reference() takes and returns one part's arrays. A program takes and returns all parts, laid end to end along the dimension named above; an argument that names none is the same for every part. Nothing has to cross between parts.
All inputs are finite; a program needn't handle non-finite values.
Results may differ from the reference program's by a relative error of at most 0.0049.
Values may be sent and summed in bfloat16 or wider, within the bound.
No kernel may reach another device: no remote copies, remote signals or barrier semaphores. Data moves between devices by JAX's collectives and lax.ppermute only.
A program may use at most 64 MiB of HBM per device.

```python
import jax
import jax.numpy as jnp
from jax import lax

C = 128
H = 128
N_RES = 192


def steps_of(stream_key, extent, split, low, top_value):
    def one(position, shards_of):
        heights = jax.random.uniform(jax.random.fold_in(jax.random.fold_in(stream_key, 6), position), (shards_of,), jnp.float32, low / len(split), top_value / len(split))
        return jnp.repeat(jnp.exp(heights), extent[position] // shards_of).reshape((-1,) + (1,) * (len(extent) - position - 1))

    level = one(*split[0])
    for cut in split[1:]:
        level = level * one(*cut)
    return level


def bell_draw(stream_key, extent, width, bound, pieces=(), kind=jnp.bfloat16):
    level = steps_of(stream_key, extent, pieces, -0.22, 0.18) if pieces else 1.0
    drawn = jax.random.normal(stream_key, extent, jnp.float32) * width * level
    return jnp.minimum(jnp.maximum(drawn, -bound), bound).astype(kind)


def setup_inputs(seed: int = 0, part: int = 0) -> dict:
    keys = jax.random.split(jax.random.key(seed), 7)
    part_keys = jax.random.split(jax.random.fold_in(keys[6], part), 7)
    pair = bell_draw(part_keys[0], (N_RES, N_RES, C), 1.0, 6.0, ((0, 64),), jnp.float32)
    norm_in = jnp.clip(1.0 + 0.18 * jax.random.normal(keys[1], (2, C), jnp.float32), 0.1, 1.9)
    w_proj = bell_draw(keys[2], (2, C, 4 * H), C ** -0.5, 0.5)
    w_gate = bell_draw(keys[3], (2, C, C), C ** -0.5, 0.5)
    norm_mid = jnp.clip(1.0 + 0.18 * jax.random.normal(keys[4], (2, H), jnp.float32), 0.1, 1.9)
    w_out = bell_draw(keys[5], (2, H, C), H ** -0.5, 0.5)
    return {"pair": pair, "norm_in": norm_in, "w_proj": w_proj, "w_gate": w_gate, "norm_mid": norm_mid, "w_out": w_out}


def layer_norm(value, gain):
    mean = lax.optimization_barrier(jnp.mean(value, axis=-1, keepdims=True))
    cent = value - mean
    var = lax.optimization_barrier(jnp.mean(cent * cent, axis=-1, keepdims=True))
    return cent / jnp.sqrt(var + 1e-05) * gain

def project(state, norm_in, w_proj, w_gate, which):
    normed = layer_norm(state, norm_in[which]).astype(jnp.bfloat16)
    proj = jnp.einsum('ijc,cd->ijd', normed.astype(jnp.float32), w_proj[which].astype(jnp.float32))
    left = (jax.nn.sigmoid(proj[..., 0:H]) * proj[..., H:2 * H]).astype(jnp.bfloat16)
    right = (jax.nn.sigmoid(proj[..., 2 * H:3 * H]) * proj[..., 3 * H:4 * H]).astype(jnp.bfloat16)
    gate = jax.nn.sigmoid(jnp.einsum('ijc,cd->ijd', normed.astype(jnp.float32), w_gate[which].astype(jnp.float32)))
    return (left, right, gate)

def finish(state, tri, gate, norm_mid, w_out, which):
    mid = layer_norm(tri, norm_mid[which]).astype(jnp.bfloat16)
    update = jnp.einsum('ijh,hc->ijc', mid.astype(jnp.float32), w_out[which].astype(jnp.float32))
    return state + gate * update

def reference(pair, norm_in, w_proj, w_gate, norm_mid, w_out):
    left, right, gate = project(pair, norm_in, w_proj, w_gate, 0)
    tri = jnp.einsum('ikh,jkh->ijh', left.astype(jnp.float32), right.astype(jnp.float32))
    state = finish(pair, tri, gate, norm_mid, w_out, 0)
    left, right, gate = project(state, norm_in, w_proj, w_gate, 1)
    tri = jnp.einsum('kih,kjh->ijh', left.astype(jnp.float32), right.astype(jnp.float32))
    return finish(state, tri, gate, norm_mid, w_out, 1)
```

```python
import jax
import jax.numpy as jnp
from jax import lax
from jax.sharding import PartitionSpec as P


def layer_norm(value, gain, axis):
    mean = jnp.mean(value, axis=axis, keepdims=True)
    cent = value - mean
    var = jnp.mean(cent * cent, axis=axis, keepdims=True)
    return cent / jnp.sqrt(var + 1e-05) * gain


def per_device(pair, norm_in, w_proj, w_gate, norm_mid, w_out):
    rows, cols, chans = pair.shape
    hidden = w_proj.shape[2] // 4
    parts = cols // rows
    own = hidden // parts

    def project(state, which):
        normed = layer_norm(state, norm_in[which], -1).astype(jnp.bfloat16)
        proj = jnp.einsum(
            "cd,ijc->dij", w_proj[which], normed, preferred_element_type=jnp.float32
        ).reshape(4, hidden, rows, cols)
        left = (jax.nn.sigmoid(proj[0]) * proj[1]).astype(jnp.bfloat16)
        right = (jax.nn.sigmoid(proj[2]) * proj[3]).astype(jnp.bfloat16)
        gate = jax.nn.sigmoid(
            jnp.einsum("ijc,cd->ijd", normed, w_gate[which], preferred_element_type=jnp.float32)
        )
        both = jnp.stack(
            [left.reshape(parts, own, rows, cols), right.reshape(parts, own, rows, cols)], axis=1
        )
        return both.reshape(parts, 2 * own, rows * cols), gate

    def to_channels(both):
        got = lax.all_to_all(both, "dap", 0, 0, tiled=True)
        got = got.reshape(parts, 2, own, rows, cols).transpose(1, 2, 0, 3, 4)
        got = got.reshape(2, own, cols, cols)
        return got[0], got[1]

    def to_rows(tri):
        send = tri.astype(jnp.bfloat16).reshape(own, parts, rows, cols).transpose(1, 0, 2, 3)
        got = lax.all_to_all(send.reshape(parts, own * rows, cols), "dap", 0, 0, tiled=True)
        return got.reshape(hidden, rows, cols).astype(jnp.float32)

    def finish(state, tri, gate, which):
        mid = layer_norm(tri, norm_mid[which][:, None, None], 0).astype(jnp.bfloat16)
        update = jnp.einsum("hij,hc->ijc", mid, w_out[which], preferred_element_type=jnp.float32)
        return state + gate * update

    both, gate = project(pair, 0)
    left, right = to_channels(both)
    tri = jnp.einsum("hik,hjk->hij", left, right, preferred_element_type=jnp.float32)
    state = finish(pair, to_rows(tri), gate, 0)
    both, gate = project(state, 1)
    left, right = to_channels(both)
    tri = jnp.einsum("hki,hkj->hij", left, right, preferred_element_type=jnp.float32)
    return finish(state, to_rows(tri), gate, 1)


def solution(mesh):
    return jax.shard_map(
        per_device,
        mesh=mesh,
        in_specs=(P(("crop", "dap"), None, None), P(), P(), P(), P(), P()),
        out_specs=P(("crop", "dap"), None, None),
        check_vma=False,
    )
```

```python
import jax
import jax.numpy as jnp
from jax import lax
from jax.experimental import pallas as pl
from jax.experimental.pallas import tpu as pltpu
from jax.sharding import PartitionSpec as P

F32 = jnp.float32
BF16 = jnp.bfloat16
LANES = 128


def column(row):
    return jnp.transpose(jnp.broadcast_to(row, (8, row.shape[1])))[:, 0:1]


def norm_rows(value, gain):
    mean = jnp.mean(value, axis=0, keepdims=True)
    cent = value - mean
    var = jnp.mean(cent * cent, axis=0, keepdims=True)
    return (cent * lax.rsqrt(var + 1e-05) * gain).astype(BF16)


def mix(weight, value):
    return lax.dot_general(weight, value, (((0,), (0,)), ((), ())), preferred_element_type=F32)


def project(state, gain, w_proj, w_gate, both, gate):
    hidden = w_gate.shape[0]
    half = hidden // 2
    normed = norm_rows(state, gain)
    for side in range(2):
        proj = mix(w_proj[:, 2 * side * hidden : 2 * (side + 1) * hidden], normed)
        edge = (jax.nn.sigmoid(proj[:hidden]) * proj[hidden:]).astype(BF16)
        both[2 * side] = edge[:half]
        both[2 * side + 1] = edge[half:]
    gate[...] = jax.nn.sigmoid(mix(w_gate, normed))


def first_kernel(pair, norm_in, w_proj, w_gate, both, gate, state):
    rows, cols, chans = pair.shape
    value = jnp.transpose(pair[...].reshape(rows * cols, chans))
    state[...] = value
    project(value, column(norm_in[0:1, :]), w_proj[0], w_gate[0], both, gate)


def finished(got, state, gate, norm_mid, w_out):
    tri = got[...].astype(F32).reshape(state.shape)
    return state[...] + gate[...] * mix(w_out, norm_rows(tri, norm_mid))


def middle_kernel(
    got, state, gate, norm_in, w_proj, w_gate, norm_mid, w_out, both, gate_next, state_next
):
    value = finished(got, state, gate, column(norm_mid[0:1, :]), w_out[0])
    state_next[...] = value
    project(value, column(norm_in[1:2, :]), w_proj[0], w_gate[0], both, gate_next)


def last_kernel(got, state, gate, norm_mid, w_out, out):
    value = finished(got, state, gate, column(norm_mid[1:2, :]), w_out[0])
    out[...] = jnp.transpose(value).reshape(out.shape)


def stacked(value, cols):
    return jnp.concatenate([value[:, k : k + cols] for k in range(0, value.shape[1], cols)], axis=0)


def outgoing_kernel(got, out, scratch):
    parts, places = got.shape[1:]
    cols = scratch.shape[1]
    rows = cols // parts
    rest = cols - LANES
    for chan in range(2):
        right = jnp.concatenate(
            [got[2 + chan].astype(F32), jnp.zeros((parts, LANES - rest), F32)], axis=1
        )
        for k in range(rows):
            for piece in range(2):
                start = k * cols + piece * LANES
                scratch[piece, pl.ds(k, parts, stride=rows), :] = right[:, start : start + LANES]
        folded = jnp.concatenate([scratch[0], scratch[1][:, :rest]], axis=1).astype(BF16)
        tri = lax.dot_general(
            stacked(got[chan], cols),
            folded,
            (((1,), (1,)), ((), ())),
            preferred_element_type=F32,
        ).astype(BF16)
        for k in range(rows):
            out[chan, :, k * cols : (k + 1) * cols] = tri[k * parts : (k + 1) * parts]


def incoming_kernel(got, out, scratch):
    parts = got.shape[1]
    cols = scratch.shape[1]
    rows = cols // parts
    rest = cols - LANES
    for chan in range(2):
        tri = mix(stacked(got[chan], cols), stacked(got[2 + chan], cols))
        scratch[0] = tri[:, :LANES]
        scratch[1] = jnp.concatenate([tri[:, LANES:], jnp.zeros((cols, LANES - rest), F32)], axis=1)
        for k in range(rows):
            picked = [scratch[piece, pl.ds(k, parts, stride=rows), :] for piece in range(2)]
            out[chan, :, k * cols : (k + 1) * cols] = jnp.concatenate(
                [picked[0], picked[1][:, :rest]], axis=1
            ).astype(BF16)


def per_device(pair, norm_in, w_proj, w_gate, norm_mid, w_out):
    rows, cols, chans = pair.shape
    hidden = w_proj.shape[2] // 4
    parts = cols // rows
    places = rows * cols
    both_t = jax.ShapeDtypeStruct((4, parts, places), BF16)
    tri_t = jax.ShapeDtypeStruct((2, parts, places), BF16)
    flat_t = jax.ShapeDtypeStruct((chans, places), F32)
    params = pltpu.CompilerParams(vmem_limit_bytes=32 * 2**20)

    def whole(shape):
        return pl.BlockSpec(shape, lambda i: (0,) * len(shape))

    def chosen(array, which):
        return pl.BlockSpec((1,) + array.shape[1:], lambda i: (which, 0, 0))

    def call(kernel, ins, in_specs, outs, scratch=()):
        return pl.pallas_call(
            kernel,
            grid=(1,),
            in_specs=in_specs,
            out_specs=[whole(o.shape) for o in outs],
            out_shape=outs,
            scratch_shapes=scratch,
            compiler_params=params,
        )(*ins)

    def exchange(value):
        return lax.all_to_all(value, "dap", 1, 1, tiled=True)

    square = [pltpu.VMEM((2, cols, LANES), F32)]
    both, gate, state = call(
        first_kernel,
        (pair, norm_in, w_proj, w_gate),
        [whole(pair.shape), whole(norm_in.shape), chosen(w_proj, 0), chosen(w_gate, 0)],
        [both_t, flat_t, flat_t],
    )
    (tri,) = call(outgoing_kernel, (exchange(both),), [whole(both_t.shape)], [tri_t], square)
    both, gate, state = call(
        middle_kernel,
        (exchange(tri), state, gate, norm_in, w_proj, w_gate, norm_mid, w_out),
        [
            whole(tri_t.shape),
            whole(flat_t.shape),
            whole(flat_t.shape),
            whole(norm_in.shape),
            chosen(w_proj, 1),
            chosen(w_gate, 1),
            whole(norm_mid.shape),
            chosen(w_out, 0),
        ],
        [both_t, flat_t, flat_t],
    )
    (tri,) = call(incoming_kernel, (exchange(both),), [whole(both_t.shape)], [tri_t], square)
    (out,) = call(
        last_kernel,
        (exchange(tri), state, gate, norm_mid, w_out),
        [
            whole(tri_t.shape),
            whole(flat_t.shape),
            whole(flat_t.shape),
            whole(norm_mid.shape),
            chosen(w_out, 1),
        ],
        [jax.ShapeDtypeStruct(pair.shape, F32)],
    )
    return out


def solution(mesh):
    return jax.shard_map(
        per_device,
        mesh=mesh,
        in_specs=(P(("crop", "dap"), None, None), P(), P(), P(), P(), P()),
        out_specs=P(("crop", "dap"), None, None),
        check_vma=False,
    )
```

```python
import jax
import jax.numpy as jnp
from jax import lax
from jax.experimental import pallas as pl
from jax.experimental.pallas import tpu as pltpu
from jax.sharding import PartitionSpec as P

F32 = jnp.float32
BF16 = jnp.bfloat16
LANES = 128


def column(row):
    return jnp.transpose(jnp.broadcast_to(row, (8, row.shape[1])))[:, 0:1]


def norm_rows(value, gain):
    mean = jnp.mean(value, axis=0, keepdims=True)
    cent = value - mean
    var = jnp.mean(cent * cent, axis=0, keepdims=True)
    return (cent * lax.rsqrt(var + 1e-05) * gain).astype(BF16)


def mix(weight, value):
    return lax.dot_general(weight, value, (((0,), (0,)), ((), ())), preferred_element_type=F32)


def project(state, gain, w_proj, both):
    hidden = w_proj.shape[1] // 4
    half = hidden // 2
    normed = norm_rows(state, gain)
    for side in range(2):
        proj = mix(w_proj[:, 2 * side * hidden : 2 * (side + 1) * hidden], normed)
        edge = (jax.nn.sigmoid(proj[:hidden]) * proj[hidden:]).astype(BF16)
        both[side] = jnp.concatenate([edge[:half], edge[half:]], axis=1)
    return normed


def first_kernel(
    pair,
    norm_in,
    w_proj,
    w_gate,
    norm_mid,
    w_out,
    both,
    gate,
    state,
    norm_in_near,
    w_proj_near,
    w_gate_near,
    norm_mid_near,
    w_out_near,
    pair_near,
    sems,
):
    rows, cols, chans = pair.shape
    moves = [
        pltpu.make_async_copy(far, near, sems.at[k])
        for k, (far, near) in enumerate(
            [
                (pair, pair_near),
                (norm_in, norm_in_near),
                (w_proj, w_proj_near),
                (w_gate, w_gate_near),
                (norm_mid, norm_mid_near),
                (w_out, w_out_near),
            ]
        )
    ]
    for move in moves:
        move.start()
    for move in moves[:3]:
        move.wait()
    value = jnp.transpose(pair_near[...].reshape(rows * cols, chans))
    state[...] = value
    normed = project(value, column(norm_in_near[0:1, :]), w_proj_near[0], both)
    moves[3].wait()
    gate[...] = jax.nn.sigmoid(mix(w_gate_near[0], normed))
    for move in moves[4:]:
        move.wait()


def middle_kernel(
    got, state, gate, norm_in, w_proj, w_gate, norm_mid, w_out, both, gate_next, state_next
):
    tri = got[...].astype(F32).reshape(state.shape)
    mid = norm_rows(tri, column(norm_mid[0:1, :]))
    value = state[...] + gate[...] * mix(w_out[0], mid)
    state_next[...] = value
    normed = project(value, column(norm_in[1:2, :]), w_proj[1], both)
    gate_next[...] = jax.nn.sigmoid(mix(w_gate[1], normed))


def last_kernel(got, state, gate, norm_mid, w_out, out, near, sems):
    rows, cols, chans = out.shape
    gain = column(norm_mid[1:2, :])
    moves = []
    for k in range(rows):
        part = slice(k * cols, (k + 1) * cols)
        tri = got[:, :, part].astype(F32).reshape(chans, cols)
        value = state[:, part] + gate[:, part] * mix(w_out[1], norm_rows(tri, gain))
        near[k] = jnp.transpose(value)
        move = pltpu.make_async_copy(near.at[k], out.at[k], sems.at[k])
        move.start()
        moves.append(move)
    for move in moves:
        move.wait()


def stacked(value, cols):
    return jnp.concatenate([value[:, k : k + cols] for k in range(0, value.shape[1], cols)], axis=0)


def outgoing_kernel(got, out, scratch):
    chans, parts, places = out.shape
    cols = scratch.shape[1]
    rows = cols // parts
    rest = cols - LANES
    for chan in range(chans):
        part = slice(chan * places, (chan + 1) * places)
        right = jnp.concatenate(
            [got[1, :, part].astype(F32), jnp.zeros((parts, LANES - rest), F32)], axis=1
        )
        for k in range(rows):
            for piece in range(2):
                start = k * cols + piece * LANES
                scratch[piece, pl.ds(k, parts, stride=rows), :] = right[:, start : start + LANES]
        folded = jnp.concatenate([scratch[0], scratch[1][:, :rest]], axis=1).astype(BF16)
        tri = lax.dot_general(
            stacked(got[0, :, part], cols),
            folded,
            (((1,), (1,)), ((), ())),
            preferred_element_type=F32,
        ).astype(BF16)
        for k in range(rows):
            out[chan, :, k * cols : (k + 1) * cols] = tri[k * parts : (k + 1) * parts]


def incoming_kernel(got, out, scratch):
    chans, parts, places = out.shape
    cols = scratch.shape[1]
    rows = cols // parts
    rest = cols - LANES
    for chan in range(chans):
        part = slice(chan * places, (chan + 1) * places)
        tri = mix(stacked(got[0, :, part], cols), stacked(got[1, :, part], cols))
        scratch[0] = tri[:, :LANES]
        scratch[1] = jnp.concatenate([tri[:, LANES:], jnp.zeros((cols, LANES - rest), F32)], axis=1)
        for k in range(rows):
            picked = [scratch[piece, pl.ds(k, parts, stride=rows), :] for piece in range(2)]
            out[chan, :, k * cols : (k + 1) * cols] = jnp.concatenate(
                [picked[0], picked[1][:, :rest]], axis=1
            ).astype(BF16)


def per_device(pair, norm_in, w_proj, w_gate, norm_mid, w_out):
    rows, cols, chans = pair.shape
    parts = cols // rows
    places = rows * cols
    both_t = jax.ShapeDtypeStruct((2, parts, 2 * places), BF16)
    tri_t = jax.ShapeDtypeStruct((2, parts, places), BF16)
    flat_t = jax.ShapeDtypeStruct((chans, places), F32)
    near = pl.BlockSpec(memory_space=pltpu.VMEM)
    far = pl.BlockSpec(memory_space=pl.ANY)
    dma = pltpu.SemaphoreType.DMA

    def call(kernel, ins, outs, scratch=(), in_spec=near, out_spec=near):
        return pl.pallas_call(
            kernel,
            in_specs=[in_spec] * len(ins),
            out_specs=[out_spec] * len(outs),
            out_shape=outs,
            scratch_shapes=scratch,
            compiler_params=pltpu.CompilerParams(vmem_limit_bytes=32 * 2**20),
        )(*ins)

    def exchange(value):
        return lax.all_to_all(value, "dap", 1, 1, tiled=True)

    def like(array):
        return jax.ShapeDtypeStruct(array.shape, array.dtype)

    square = [pltpu.VMEM((2, cols, LANES), F32)]
    params = (norm_in, w_proj, w_gate, norm_mid, w_out)
    both, gate, state, *params = call(
        first_kernel,
        tuple(pltpu.with_memory_space_constraint(a, pltpu.HBM) for a in (pair, *params)),
        [both_t, flat_t, flat_t, *map(like, params)],
        [pltpu.VMEM(pair.shape, F32), dma((6,))],
        in_spec=far,
    )
    norm_mid, w_out = params[3:]
    (tri,) = call(outgoing_kernel, (exchange(both),), [tri_t], square)
    both, gate, state = call(
        middle_kernel, (exchange(tri), state, gate, *params), [both_t, flat_t, flat_t]
    )
    (tri,) = call(incoming_kernel, (exchange(both),), [tri_t], square)
    (out,) = call(
        last_kernel,
        (exchange(tri), state, gate, norm_mid, w_out),
        [like(pair)],
        [pltpu.VMEM(pair.shape, F32), dma((rows,))],
        out_spec=far,
    )
    return out


def solution(mesh):
    return jax.shard_map(
        per_device,
        mesh=mesh,
        in_specs=(P(("crop", "dap"), None, None), P(), P(), P(), P(), P()),
        out_specs=P(("crop", "dap"), None, None),
        check_vma=False,
    )
```

```python
import math

import jax
import jax.numpy as jnp
from jax import lax
from jax.experimental import pallas as pl
from jax.experimental.pallas import tpu as pltpu
from jax.sharding import PartitionSpec as P

F32 = jnp.float32
BF16 = jnp.bfloat16


def column(row):
    return jnp.transpose(jnp.broadcast_to(row, (8, row.shape[1])))[:, 0:1]


def norm_rows(value, gain):
    mean = jnp.mean(value, axis=0, keepdims=True)
    cent = value - mean
    var = jnp.mean(cent * cent, axis=0, keepdims=True)
    return (cent * lax.rsqrt(var + 1e-05) * gain).astype(BF16)


def mix(weight, value):
    return lax.dot_general(weight, value, (((0,), (0,)), ((), ())), preferred_element_type=F32)


def sigmoid(value):
    return 0.5 * jnp.tanh(0.5 * value) + 0.5


def project(state, gain, w_proj, both):
    hidden = w_proj.shape[1] // 4
    half = hidden // 2
    normed = norm_rows(state, gain)
    for side in range(2):
        proj = mix(w_proj[:, 2 * side * hidden : 2 * (side + 1) * hidden], normed)
        edge = (sigmoid(proj[:hidden]) * proj[hidden:]).astype(BF16)
        both[side] = jnp.concatenate([edge[:half], edge[half:]], axis=1)
    return normed


def first_kernel(
    pair,
    norm_in,
    w_proj,
    w_gate,
    norm_mid,
    w_out,
    both,
    gate,
    state,
    norm_in_near,
    w_proj_near,
    w_gate_near,
    norm_mid_near,
    w_out_near,
    pair_near,
    sems,
):
    rows, cols, chans = pair.shape
    half = cols // 2
    pairs = [
        (norm_in, norm_in_near),
        *((pair.at[k, pl.ds(h, half)], pair_near.at[k, pl.ds(h, half)]) for k in range(rows) for h in (0, half)),
        (w_proj.at[0], w_proj_near.at[0]),
        (w_gate, w_gate_near),
        (w_proj.at[1], w_proj_near.at[1]),
        (norm_mid, norm_mid_near),
        (w_out, w_out_near),
    ]
    moves = [pltpu.make_async_copy(*ends, sems.at[k]) for k, ends in enumerate(pairs)]
    for move in moves:
        move.start()
    for move in moves[:7]:
        move.wait()
    parts = cols // rows
    value = jnp.transpose(
        jnp.concatenate(
            [
                pair_near[k, pl.ds(j, parts, stride=rows), :]
                for k in range(rows)
                for j in range(rows)
            ],
            axis=0,
        )
    )
    state[...] = value
    gain = column(norm_in_near[0:1, :])
    moves[7].wait()
    normed = project(value, gain, w_proj_near[0], both)
    moves[8].wait()
    gate[...] = sigmoid(mix(w_gate_near[0], normed))
    for move in moves[9:]:
        move.wait()


def middle_kernel(
    got, state, gate, norm_in, w_proj, w_gate, norm_mid, w_out, both, gate_next, state_next
):
    tri = got[...].astype(F32).reshape(state.shape)
    mid = norm_rows(tri, column(norm_mid[0:1, :]))
    value = state[...] + gate[...] * mix(w_out[0], mid)
    state_next[...] = value
    normed = project(value, column(norm_in[1:2, :]), w_proj[1], both)
    gate_next[...] = sigmoid(mix(w_gate[1], normed))


def last_kernel(got, state, gate, norm_mid, w_out, out, near, sems):
    rows, cols, chans = out.shape
    parts = cols // rows
    gain = column(norm_mid[1:2, :])
    moves = []
    for k, stop in ((0, rows - 1), (rows - 1, rows)):
        part = slice(k * cols, stop * cols)
        tri = got[:, :, part].astype(F32).reshape(chans, -1)
        value = state[:, part] + gate[:, part] * mix(w_out[1], norm_rows(tri, gain))
        block = pl.ds(k, stop - k)
        turned = jnp.transpose(value)
        for piece in range((stop - k) * rows):
            near[k + piece // rows, pl.ds(piece % rows, parts, stride=rows), :] = turned[
                piece * parts : (piece + 1) * parts
            ]
        move = pltpu.make_async_copy(near.at[block], out.at[block], sems.at[len(moves)])
        move.start()
        moves.append(move)
    for move in moves:
        move.wait()


def stacked(value, cols):
    return jnp.concatenate([value[:, k : k + cols] for k in range(0, value.shape[1], cols)], axis=0)


def product(got, out, dims):
    chans, parts, places = out.shape
    cols = math.isqrt(parts * places)
    for chan in range(chans):
        part = slice(chan * places, (chan + 1) * places)
        left, right = (stacked(got[side, :, part], cols) for side in range(2))
        tri = lax.dot_general(left, right, (dims, ((), ())), preferred_element_type=F32)
        tri = tri.astype(BF16)
        out[chan] = jnp.concatenate([tri[k : k + parts] for k in range(0, cols, parts)], axis=1)


def outgoing_kernel(got, out):
    product(got, out, ((1,), (1,)))


def incoming_kernel(got, out):
    product(got, out, ((0,), (0,)))


def per_device(pair, norm_in, w_proj, w_gate, norm_mid, w_out):
    rows, cols, chans = pair.shape
    parts = cols // rows
    places = rows * cols
    both_t = jax.ShapeDtypeStruct((2, parts, 2 * places), BF16)
    tri_t = jax.ShapeDtypeStruct((2, parts, places), BF16)
    flat_t = jax.ShapeDtypeStruct((chans, places), F32)
    near = pl.BlockSpec(memory_space=pltpu.VMEM)
    far = pl.BlockSpec(memory_space=pl.ANY)
    dma = pltpu.SemaphoreType.DMA

    def call(kernel, ins, outs, scratch=(), in_spec=near, out_spec=near):
        return pl.pallas_call(
            kernel,
            in_specs=[in_spec] * len(ins),
            out_specs=[out_spec] * len(outs),
            out_shape=outs,
            scratch_shapes=scratch,
            compiler_params=pltpu.CompilerParams(vmem_limit_bytes=32 * 2**20),
        )(*ins)

    def exchange(value):
        return lax.all_to_all(value, "dap", 1, 1, tiled=True)

    def like(array):
        return jax.ShapeDtypeStruct(array.shape, array.dtype)

    params = (norm_in, w_proj, w_gate, norm_mid, w_out)
    both, gate, state, *params = call(
        first_kernel,
        tuple(pltpu.with_memory_space_constraint(a, pltpu.HBM) for a in (pair, *params)),
        [both_t, flat_t, flat_t, *map(like, params)],
        [pltpu.VMEM(pair.shape, F32), dma((12,))],
        in_spec=far,
    )
    norm_mid, w_out = params[3:]
    (tri,) = call(outgoing_kernel, (exchange(both),), [tri_t])
    both, gate, state = call(
        middle_kernel, (exchange(tri), state, gate, *params), [both_t, flat_t, flat_t]
    )
    (tri,) = call(incoming_kernel, (exchange(both),), [tri_t])
    (out,) = call(
        last_kernel,
        (exchange(tri), state, gate, norm_mid, w_out),
        [like(pair)],
        [pltpu.VMEM(pair.shape, F32), dma((2,))],
        out_spec=far,
    )
    return out


def solution(mesh):
    return jax.shard_map(
        per_device,
        mesh=mesh,
        in_specs=(P(("crop", "dap"), None, None), P(), P(), P(), P(), P()),
        out_specs=P(("crop", "dap"), None, None),
        check_vma=False,
    )
```

```python
import math

import jax
import jax.numpy as jnp
from jax import lax
from jax.experimental import pallas as pl
from jax.experimental.pallas import tpu as pltpu
from jax.sharding import PartitionSpec as P

F32 = jnp.float32
BF16 = jnp.bfloat16
SCALE = 2.0**-6


def column(row):
    return jnp.transpose(jnp.broadcast_to(row, (8, row.shape[1])))[:, 0:1]


def norm_rows(value, gain):
    mean = jnp.mean(value, axis=0, keepdims=True)
    cent = value - mean
    var = jnp.mean(cent * cent, axis=0, keepdims=True)
    return (cent * lax.rsqrt(var + 1e-05) * gain).astype(BF16)


def mix(weight, value):
    return lax.dot_general(weight, value, (((0,), (0,)), ((), ())), preferred_element_type=F32)


def sigmoid(value):
    return 0.5 * jnp.tanh(0.5 * value) + 0.5


def project(state, gain, w_proj, both):
    hidden = w_proj.shape[1] // 4
    half = hidden // 2
    normed = norm_rows(state, gain)
    for side in range(2):
        proj = mix(w_proj[:, 2 * side * hidden : 2 * (side + 1) * hidden], normed)
        edge = (sigmoid(proj[:hidden]) * proj[hidden:]).astype(BF16)
        both[side] = jnp.concatenate([edge[:half], edge[half:]], axis=1)
    return normed


def first_kernel(
    pair,
    norm_in,
    w_proj,
    w_gate,
    norm_mid,
    w_out,
    both,
    gate,
    state,
    norm_in_near,
    w_proj_near,
    w_gate_near,
    norm_mid_near,
    w_out_near,
    pair_near,
    sems,
):
    rows, cols, chans = pair.shape
    half = cols // 2
    pairs = [
        (norm_in, norm_in_near),
        *((pair.at[k, pl.ds(h, half)], pair_near.at[k, pl.ds(h, half)]) for k in range(rows) for h in (0, half)),
        (w_proj.at[0], w_proj_near.at[0]),
        (w_gate, w_gate_near),
        (w_proj.at[1], w_proj_near.at[1]),
        (norm_mid, norm_mid_near),
        (w_out, w_out_near),
    ]
    moves = [pltpu.make_async_copy(*ends, sems.at[k]) for k, ends in enumerate(pairs)]
    for move in moves:
        move.start()
    for move in moves[:7]:
        move.wait()
    parts = cols // rows
    value = jnp.transpose(
        jnp.concatenate(
            [
                pair_near[k, pl.ds(j, parts, stride=rows), :]
                for k in range(rows)
                for j in range(rows)
            ],
            axis=0,
        )
    )
    state[...] = value
    gain = column(norm_in_near[0:1, :])
    moves[7].wait()
    normed = project(value, gain, w_proj_near[0], both)
    moves[8].wait()
    gate[...] = sigmoid(mix(w_gate_near[0], normed))
    for move in moves[9:]:
        move.wait()


def middle_kernel(
    got, state, gate, norm_in, w_proj, w_gate, norm_mid, w_out, both, gate_next, state_next
):
    tri = got[...].reshape(state.shape)
    mid = norm_rows(tri, column(norm_mid[0:1, :]))
    value = state[...] + gate[...] * mix(w_out[0], mid)
    state_next[...] = value
    normed = project(value, column(norm_in[1:2, :]), w_proj[1], both)
    gate_next[...] = sigmoid(mix(w_gate[1], normed))


def last_kernel(got, state, gate, norm_mid, w_out, out, near, sems):
    rows, cols, chans = out.shape
    parts = cols // rows
    gain = column(norm_mid[1:2, :])
    moves = []
    for k, stop in ((0, rows - 1), (rows - 1, rows)):
        part = slice(k * cols, stop * cols)
        tri = got[:, :, part].reshape(chans, -1)
        value = state[:, part] + gate[:, part] * mix(w_out[1], norm_rows(tri, gain))
        block = pl.ds(k, stop - k)
        turned = jnp.transpose(value)
        for piece in range((stop - k) * rows):
            near[k + piece // rows, pl.ds(piece % rows, parts, stride=rows), :] = turned[
                piece * parts : (piece + 1) * parts
            ]
        move = pltpu.make_async_copy(near.at[block], out.at[block], sems.at[len(moves)])
        move.start()
        moves.append(move)
    for move in moves:
        move.wait()


def stacked(value, cols):
    return jnp.concatenate([value[:, k : k + cols] for k in range(0, value.shape[1], cols)], axis=0)


def product(got, out, dims):
    chans, parts, places = out.shape
    cols = math.isqrt(parts * places)
    for chan in range(chans):
        part = slice(chan * places, (chan + 1) * places)
        left, right = (stacked(got[side, :, part], cols) for side in range(2))
        tri = lax.dot_general(left, right, (dims, ((), ())), preferred_element_type=F32)
        out[chan] = jnp.concatenate([tri[k : k + parts] for k in range(0, cols, parts)], axis=1)


def outgoing_kernel(got, out):
    product(got, out, ((1,), (1,)))


def incoming_kernel(got, out):
    product(got, out, ((0,), (0,)))


def per_device(pair, norm_in, w_proj, w_gate, norm_mid, w_out):
    rows, cols, chans = pair.shape
    parts = cols // rows
    places = rows * cols
    both_t = jax.ShapeDtypeStruct((2, parts, 2 * places), BF16)
    tri_t = jax.ShapeDtypeStruct((2, parts, places), F32)
    flat_t = jax.ShapeDtypeStruct((chans, places), F32)
    near = pl.BlockSpec(memory_space=pltpu.VMEM)
    far = pl.BlockSpec(memory_space=pl.ANY)
    dma = pltpu.SemaphoreType.DMA

    def call(kernel, ins, outs, scratch=(), in_spec=near, out_spec=near):
        return pl.pallas_call(
            kernel,
            in_specs=[in_spec] * len(ins),
            out_specs=[out_spec] * len(outs),
            out_shape=outs,
            scratch_shapes=scratch,
            compiler_params=pltpu.CompilerParams(vmem_limit_bytes=32 * 2**20),
        )(*ins)

    def exchange(value):
        return lax.all_to_all(value, "dap", 1, 1, tiled=True)

    def exchange_half(value):
        value = exchange((value * SCALE).astype(jnp.float16))
        return value.astype(F32) * (1 / SCALE)

    def like(array):
        return jax.ShapeDtypeStruct(array.shape, array.dtype)

    params = (norm_in, w_proj, w_gate, norm_mid, w_out)
    both, gate, state, *params = call(
        first_kernel,
        tuple(pltpu.with_memory_space_constraint(a, pltpu.HBM) for a in (pair, *params)),
        [both_t, flat_t, flat_t, *map(like, params)],
        [pltpu.VMEM(pair.shape, F32), dma((12,))],
        in_spec=far,
    )
    norm_mid, w_out = params[3:]
    (tri,) = call(outgoing_kernel, (exchange(both),), [tri_t])
    both, gate, state = call(
        middle_kernel, (exchange_half(tri), state, gate, *params), [both_t, flat_t, flat_t]
    )
    (tri,) = call(incoming_kernel, (exchange(both),), [tri_t])
    (out,) = call(
        last_kernel,
        (exchange_half(tri), state, gate, norm_mid, w_out),
        [like(pair)],
        [pltpu.VMEM(pair.shape, F32), dma((2,))],
        out_spec=far,
    )
    return out


def solution(mesh):
    return jax.shard_map(
        per_device,
        mesh=mesh,
        in_specs=(P(("crop", "dap"), None, None), P(), P(), P(), P(), P()),
        out_specs=P(("crop", "dap"), None, None),
        check_vma=False,
    )
```

```python
import math

import jax
import jax.numpy as jnp
from jax import lax
from jax.experimental import pallas as pl
from jax.experimental.pallas import tpu as pltpu
from jax.sharding import PartitionSpec as P

F32 = jnp.float32
BF16 = jnp.bfloat16
SCALE = 2.0**-6
LANES = 128


def column(row):
    return jnp.transpose(jnp.broadcast_to(row, (8, row.shape[1])))[:, 0:1]


def norm_rows(value, gain):
    mean = jnp.mean(value, axis=0, keepdims=True)
    cent = value - mean
    var = jnp.mean(cent * cent, axis=0, keepdims=True)
    return (cent * lax.rsqrt(var + 1e-05) * gain).astype(BF16)


def mix(weight, value):
    return lax.dot_general(weight, value, (((0,), (0,)), ((), ())), preferred_element_type=F32)


def sigmoid(value):
    return 0.5 * jnp.tanh(0.5 * value) + 0.5


def edge(proj):
    hidden = proj.shape[0] // 2
    return (sigmoid(proj[:hidden]) * proj[hidden:]).astype(BF16)


def first_kernel(
    pair,
    norm_in,
    w_proj,
    w_gate,
    norm_mid,
    w_out,
    both,
    gate,
    state,
    norm_in_near,
    w_proj_near,
    w_gate_near,
    norm_mid_near,
    w_out_near,
    pair_near,
    sems,
):
    rows, cols, chans = pair.shape
    half = cols // 2
    pairs = [
        (norm_in, norm_in_near),
        *((pair.at[k, pl.ds(h, half)], pair_near.at[k, pl.ds(h, half)]) for k in range(rows) for h in (0, half)),
        (w_proj.at[0], w_proj_near.at[0]),
        (w_gate, w_gate_near),
        (w_proj.at[1], w_proj_near.at[1]),
        (norm_mid, norm_mid_near),
        (w_out, w_out_near),
    ]
    moves = [pltpu.make_async_copy(*ends, sems.at[k]) for k, ends in enumerate(pairs)]
    for move in moves:
        move.start()
    for move in moves[:7]:
        move.wait()
    parts = cols // rows
    value = jnp.transpose(
        jnp.concatenate(
            [
                pair_near[k, pl.ds(j, parts, stride=rows), :]
                for k in range(rows)
                for j in range(rows)
            ],
            axis=0,
        )
    )
    state[...] = value
    gain = column(norm_in_near[0:1, :])
    moves[7].wait()
    moves[8].wait()
    normed = norm_rows(value, gain)
    weights = jnp.concatenate([w_proj_near[0], w_gate_near[0]], axis=1)
    proj = mix(weights, normed)
    both[...] = jnp.concatenate(
        [edge(proj[: 2 * chans]), edge(proj[2 * chans : 4 * chans])], axis=1
    )
    gate[...] = sigmoid(proj[4 * chans :])
    for move in moves[9:]:
        move.wait()


def middle_kernel(
    got, state, gate, norm_in, w_proj, w_gate, gains, w_out, both, gate_next, state_next
):
    tri = got[...]
    mid = norm_rows(tri, gains[0][:, 0:1])
    value = state[...] + gate[...] * mix(w_out[0], mid)
    state_next[...] = value
    normed = norm_rows(value, column(norm_in[1:2, :]))
    wide = w_proj.shape[2] // 2
    both[...] = jnp.concatenate(
        [edge(mix(w_proj[1][:, :wide], normed)), edge(mix(w_proj[1][:, wide:], normed))], axis=1
    )
    gate_next[...] = sigmoid(mix(w_gate[1], normed))


def last_kernel(got, state, gate, gains, w_out, out, near, sems):
    rows, cols, chans = out.shape
    parts = cols // rows
    gain = gains[1][:, 0:1]
    moves = []
    for k, stop in ((0, rows - 1), (rows - 1, rows)):
        part = slice(k * cols, stop * cols)
        tri = got[:, part]
        value = state[:, part] + gate[:, part] * mix(w_out[1], norm_rows(tri, gain))
        block = pl.ds(k, stop - k)
        turned = jnp.transpose(value)
        for piece in range((stop - k) * rows):
            near[k + piece // rows, pl.ds(piece % rows, parts, stride=rows), :] = turned[
                piece * parts : (piece + 1) * parts
            ]
        move = pltpu.make_async_copy(near.at[block], out.at[block], sems.at[len(moves)])
        move.start()
        moves.append(move)
    for move in moves:
        move.wait()


def stacked(value, cols):
    return jnp.concatenate([value[:, k : k + cols] for k in range(0, value.shape[1], cols)], axis=0)


def product(got, out, scratch, dims):
    chans, parts, lanes = got.shape
    places = lanes // 2
    cols = math.isqrt(parts * places)
    spare = jnp.zeros((parts, scratch.shape[0] * LANES - places), F32)
    for chan in range(chans):
        left, right = (
            stacked(got[chan, :, side * places : (side + 1) * places], cols) for side in range(2)
        )
        tri = lax.dot_general(left, right, (dims, ((), ())), preferred_element_type=F32)
        tri = [tri[k : k + parts] for k in range(0, cols, parts)]
        tri = jnp.concatenate([*tri, spare], axis=1)
        for k in range(scratch.shape[0]):
            scratch[k, pl.ds(chan, parts, stride=chans), :] = tri[:, k * LANES : (k + 1) * LANES]
    tri = jnp.concatenate([scratch[k] for k in range(scratch.shape[0])], axis=1)
    out[...] = tri[:, :places]


def outgoing_kernel(got, norm_mid, w_out, out, gains, w_out_turned, tiles, scratch):
    product(got, out, tiles, ((1,), (1,)))
    half = scratch.shape[0] // 2
    for which in range(2):
        gain = jnp.broadcast_to(norm_mid[which : which + 1, :], scratch.shape)
        for value, turned in ((jnp.transpose(gain), gains), (w_out[which].astype(F32), w_out_turned)):
            scratch[...] = value
            for slot in range(2):
                turned[which, slot * half : (slot + 1) * half] = scratch[
                    pl.ds(slot, half, stride=2), :
                ].astype(turned.dtype)


def incoming_kernel(got, out, tiles):
    product(got, out, tiles, ((0,), (0,)))


def per_device(pair, norm_in, w_proj, w_gate, norm_mid, w_out):
    rows, cols, chans = pair.shape
    parts = cols // rows
    places = rows * cols
    both_t = jax.ShapeDtypeStruct((chans, 2 * places), BF16)
    tri_t = jax.ShapeDtypeStruct((chans, places), F32)
    tiles = pltpu.VMEM((pl.cdiv(places, LANES), chans, LANES), F32)
    flat_t = jax.ShapeDtypeStruct((chans, places), F32)
    near = pl.BlockSpec(memory_space=pltpu.VMEM)
    far = pl.BlockSpec(memory_space=pl.ANY)
    dma = pltpu.SemaphoreType.DMA

    def call(kernel, ins, outs, scratch=(), in_spec=near, out_spec=near):
        return pl.pallas_call(
            kernel,
            in_specs=[in_spec] * len(ins),
            out_specs=[out_spec] * len(outs),
            out_shape=outs,
            scratch_shapes=scratch,
            compiler_params=pltpu.CompilerParams(vmem_limit_bytes=32 * 2**20),
        )(*ins)

    def to_channels(both):
        both = both.reshape(parts, 2, 2 * places)
        return jnp.swapaxes(lax.all_to_all(both, "dap", 0, 0, tiled=True), 0, 1)

    def to_rows(tri):
        tri = (tri * SCALE).astype(jnp.float16).reshape(parts, 2, places)
        tri = jnp.swapaxes(lax.all_to_all(tri, "dap", 0, 0, tiled=True), 0, 1)
        tri = lax.optimization_barrier(tri)
        return tri.astype(F32).reshape(chans, places) * (1 / SCALE)

    def like(array):
        return jax.ShapeDtypeStruct(array.shape, array.dtype)

    params = (norm_in, w_proj, w_gate, norm_mid, w_out)
    both, gate, state, *params = call(
        first_kernel,
        tuple(pltpu.with_memory_space_constraint(a, pltpu.HBM) for a in (pair, *params)),
        [both_t, flat_t, flat_t, *map(like, params)],
        [pltpu.VMEM(pair.shape, F32), dma((12,))],
        in_spec=far,
    )
    tri, gains, w_out = call(
        outgoing_kernel,
        (to_channels(both), *params[3:]),
        [tri_t, jax.ShapeDtypeStruct(w_out.shape, F32), like(w_out)],
        [tiles, pltpu.VMEM(w_out.shape[1:], F32)],
    )
    both, gate, state = call(
        middle_kernel, (to_rows(tri), state, gate, *params[:3], gains, w_out), [both_t, flat_t, flat_t]
    )
    (tri,) = call(incoming_kernel, (to_channels(both),), [tri_t], [tiles])
    (out,) = call(
        last_kernel,
        (to_rows(tri), state, gate, gains, w_out),
        [like(pair)],
        [pltpu.VMEM(pair.shape, F32), dma((2,))],
        out_spec=far,
    )
    return out


def solution(mesh):
    return jax.shard_map(
        per_device,
        mesh=mesh,
        in_specs=(P(("crop", "dap"), None, None), P(), P(), P(), P(), P()),
        out_specs=P(("crop", "dap"), None, None),
        check_vma=False,
    )
```

```python
import jax
import jax.numpy as jnp
from jax import lax
from jax.experimental import pallas as pl
from jax.experimental.pallas import tpu as pltpu
from jax.sharding import PartitionSpec as P

F32 = jnp.float32
BF16 = jnp.bfloat16
LANES = 128
TOP = 2.0**14


def column(row):
    return jnp.transpose(jnp.broadcast_to(row, (8, row.shape[1])))[:, 0:1]


def norm_rows(value, gain):
    mean = jnp.mean(value, axis=0, keepdims=True)
    cent = value - mean
    var = jnp.mean(cent * cent, axis=0, keepdims=True)
    return (cent * lax.rsqrt(var + 1e-05) * gain).astype(BF16)


def mix(weight, value):
    return lax.dot_general(weight, value, (((0,), (0,)), ((), ())), preferred_element_type=F32)


def sigmoid(value):
    return 0.5 * jnp.tanh(0.5 * value) + 0.5


def blocks(rows):
    return [(k, j) for k in range(rows) for j in range(rows - 1)] + [
        (k, rows - 1) for k in range(rows)
    ]


def store_edges(both, proj):
    hidden = proj[0].shape[0] // 2
    left, right = ((sigmoid(p[:hidden]) * p[hidden:]).astype(BF16) for p in proj)
    whole = left.shape[1] // LANES * LANES
    both[:, :whole] = left[:, :whole]
    both[:, whole : whole + LANES] = jnp.concatenate([left[:, whole:], right[:, whole:]], axis=1)
    both[:, whole + LANES :] = right[:, :whole]


def first_kernel(
    pair,
    norm_in,
    w_proj,
    w_gate,
    norm_mid,
    w_out,
    both,
    normed,
    state,
    norm_in_near,
    w_proj_near,
    w_gate_near,
    norm_mid_near,
    w_out_near,
    pair_near,
    sems,
):
    rows, cols, chans = pair.shape
    half = cols // 2
    pairs = [
        (norm_in, norm_in_near),
        *((pair.at[k, pl.ds(h, half)], pair_near.at[k, pl.ds(h, half)]) for k in range(rows) for h in (0, half)),
        (w_proj.at[0], w_proj_near.at[0]),
        (w_gate, w_gate_near),
        (w_proj.at[1], w_proj_near.at[1]),
        (norm_mid, norm_mid_near),
        (w_out, w_out_near),
    ]
    moves = [pltpu.make_async_copy(*ends, sems.at[k]) for k, ends in enumerate(pairs)]
    for move in moves:
        move.start()
    for move in moves[:7]:
        move.wait()
    parts = cols // rows
    value = jnp.transpose(
        jnp.concatenate(
            [
                pair_near[k, pl.ds(j, parts, stride=rows), :] for k, j in blocks(rows)
            ],
            axis=0,
        )
    )
    state[...] = value
    gain = column(norm_in_near[0:1, :])
    moves[7].wait()
    normed[...] = norm_rows(value, gain)
    proj = mix(w_proj_near[0], normed[...])
    store_edges(both, (proj[: 2 * chans], proj[2 * chans :]))
    for move in moves[8:]:
        move.wait()


def middle_kernel(
    got, state, gate, norm_in, w_proj, gains, units, w_out, both, normed, state_next
):
    mid = norm_rows(got[...] * units[0][:, 0:1], gains[0][:, 0:1])
    value = state[...] + gate[...] * mix(w_out[0], mid)
    state_next[...] = value
    normed[...] = norm_rows(value, column(norm_in[1:2, :]))
    wide = w_proj.shape[2] // 2
    store_edges(both, [mix(w_proj[1][:, k : k + wide], normed[...]) for k in (0, wide)])


def last_kernel(got, state, gate, gains, units, w_out, out, near, sems):
    rows, cols, chans = out.shape
    parts = cols // rows
    gain = gains[1][:, 0:1]
    unit = units[1][:, 0:1]
    order = blocks(rows)
    moves = []
    for k, stop in ((0, rows - 1), (rows - 1, rows)):
        mine = [n for n, (row, _) in enumerate(order) if k <= row < stop]

        def lanes(ref):
            return jnp.concatenate([ref[:, n * parts : (n + 1) * parts] for n in mine], axis=1)

        value = lanes(state) + lanes(gate) * mix(w_out[1], norm_rows(lanes(got) * unit, gain))
        turned = jnp.transpose(value)
        for place, n in enumerate(mine):
            row, slot = order[n]
            near[row, pl.ds(slot, parts, stride=rows), :] = turned[
                place * parts : (place + 1) * parts
            ]
        block = pl.ds(k, stop - k)
        move = pltpu.make_async_copy(near.at[block], out.at[block], sems.at[len(moves)])
        move.start()
        moves.append(move)
    for move in moves:
        move.wait()


def square(value, whole, last):
    rows = [value[:, k : k + LANES] for k in range(whole, whole + 3 * LANES, LANES)]
    tail = value[:, whole + 3 * LANES : whole + 4 * LANES]
    half = LANES // 2
    tails = [tail[:, :half], tail[:, half:], last]
    return jnp.concatenate(
        [jnp.concatenate([row, end], axis=1) for row, end in zip(rows, tails)], axis=0
    )


def product(got, scales, out, tiles, dims):
    chans, parts, lanes = got.shape
    places = lanes // 2
    whole = places // LANES * LANES
    spare = jnp.zeros((parts, LANES - parts), F32)
    first = chans * lax.axis_index("dap")
    for chan in range(chans):
        value = got[chan]
        middle = value[:, whole : whole + LANES]
        left = square(value, 0, middle[:, :parts])
        right = square(value, whole + LANES, middle[:, parts:])
        tri = lax.dot_general(left, right, (dims, ((), ())), preferred_element_type=F32)
        tri = [tri[k : k + parts] for k in range(0, tri.shape[0], parts)]
        ends = [row[:, LANES:] for row in tri] + [spare]
        pieces = [row[:, :LANES] for row in tri]
        pieces += [jnp.concatenate(ends[k : k + 2], axis=1) for k in (0, 2)]
        scale = scales[pl.ds(first + chan, 1), :]
        for k, piece in enumerate(pieces):
            tiles[k, pl.ds(chan, parts, stride=chans), :] = piece * scale
    tri = jnp.concatenate([tiles[k] for k in range(tiles.shape[0])], axis=1)
    out[...] = tri[:, :places]


def largest(gain, w_proj, cols):
    hidden = w_proj.shape[1] // 4
    weighted = [
        gain * w_proj[:, k : k + hidden].astype(F32) for k in (hidden, 3 * hidden)
    ]
    left, right = (jnp.sum(w * w, axis=0, keepdims=True) for w in weighted)
    return 1.02 * cols * hidden * jnp.sqrt(left * right) + 1e-20


def outgoing_kernel(
    got,
    normed,
    norm_in,
    w_proj,
    w_gate,
    norm_mid,
    w_out,
    out,
    gate,
    gains,
    units,
    w_out_turned,
    scales,
    tiles,
    scratch,
):
    parts = got.shape[1]
    cols = 3 * parts
    half = scratch.shape[0] // 2

    def wide(row):
        return jnp.transpose(jnp.broadcast_to(row, scratch.shape))

    def turn(value, turned, which):
        scratch[...] = value
        for slot in range(2):
            turned[which, slot * half : (slot + 1) * half] = scratch[
                pl.ds(slot, half, stride=2), :
            ].astype(turned.dtype)

    for which in range(2):
        bound = largest(wide(norm_in[which : which + 1, :]), w_proj[which], cols)
        scales[which] = wide(TOP / bound)
        turn(wide(bound * (1 / TOP)), units, which)
        turn(wide(norm_mid[which : which + 1, :]), gains, which)
        turn(w_out[which].astype(F32), w_out_turned, which)
    product(got, scales.at[0], out, tiles, ((1,), (1,)))
    gate[...] = sigmoid(mix(w_gate[0], normed[...]))


def incoming_kernel(got, normed, w_gate, scales, out, gate, tiles):
    product(got, scales.at[1], out, tiles, ((0,), (0,)))
    gate[...] = sigmoid(mix(w_gate[1], normed[...]))


def per_device(pair, norm_in, w_proj, w_gate, norm_mid, w_out):
    rows, cols, chans = pair.shape
    parts = cols // rows
    places = rows * cols
    both_t = jax.ShapeDtypeStruct((chans, 2 * places), BF16)
    tri_t = jax.ShapeDtypeStruct((chans, places), F32)
    tiles = pltpu.VMEM((pl.cdiv(places, LANES), chans, LANES), F32)
    flat_t = jax.ShapeDtypeStruct((chans, places), F32)
    normed_t = jax.ShapeDtypeStruct((chans, places), BF16)
    near = pl.BlockSpec(memory_space=pltpu.VMEM)
    far = pl.BlockSpec(memory_space=pl.ANY)
    dma = pltpu.SemaphoreType.DMA

    def call(kernel, ins, outs, scratch=(), in_spec=near, out_spec=near):
        return pl.pallas_call(
            kernel,
            in_specs=[in_spec] * len(ins),
            out_specs=[out_spec] * len(outs),
            out_shape=outs,
            scratch_shapes=scratch,
            compiler_params=pltpu.CompilerParams(vmem_limit_bytes=32 * 2**20),
        )(*ins)

    def to_channels(both):
        both = both.reshape(parts, 2, 2 * places)
        return jnp.swapaxes(lax.all_to_all(both, "dap", 0, 0, tiled=True), 0, 1)

    def to_rows(tri):
        tri = tri.astype(jnp.float16).reshape(parts, 2, places)
        tri = jnp.swapaxes(lax.all_to_all(tri, "dap", 0, 0, tiled=True), 0, 1)
        tri = lax.optimization_barrier(tri)
        return tri.astype(F32).reshape(chans, places)

    def like(array):
        return jax.ShapeDtypeStruct(array.shape, array.dtype)

    params = (norm_in, w_proj, w_gate, norm_mid, w_out)
    both, normed, state, norm_in, w_proj, w_gate, norm_mid, w_out = call(
        first_kernel,
        tuple(pltpu.with_memory_space_constraint(a, pltpu.HBM) for a in (pair, *params)),
        [both_t, normed_t, flat_t, *map(like, params)],
        [pltpu.VMEM(pair.shape, F32), dma((12,))],
        in_spec=far,
    )
    wide_t = jax.ShapeDtypeStruct(w_out.shape, F32)
    tri, gate, gains, units, w_out, scales = call(
        outgoing_kernel,
        (to_channels(both), normed, norm_in, w_proj, w_gate, norm_mid, w_out),
        [tri_t, flat_t, wide_t, wide_t, like(w_out), wide_t],
        [tiles, pltpu.VMEM(w_out.shape[1:], F32)],
    )
    both, normed, state = call(
        middle_kernel,
        (to_rows(tri), state, gate, norm_in, w_proj, gains, units, w_out),
        [both_t, normed_t, flat_t],
    )
    tri, gate = call(
        incoming_kernel, (to_channels(both), normed, w_gate, scales), [tri_t, flat_t], [tiles]
    )
    (out,) = call(
        last_kernel,
        (to_rows(tri), state, gate, gains, units, w_out),
        [like(pair)],
        [pltpu.VMEM(pair.shape, F32), dma((2,))],
        out_spec=far,
    )
    return out


def solution(mesh):
    return jax.shard_map(
        per_device,
        mesh=mesh,
        in_specs=(P(("crop", "dap"), None, None), P(), P(), P(), P(), P()),
        out_specs=P(("crop", "dap"), None, None),
        check_vma=False,
    )
```

```python
import jax
import jax.numpy as jnp
from jax import lax
from jax.experimental import pallas as pl
from jax.experimental.pallas import tpu as pltpu
from jax.sharding import PartitionSpec as P

F32 = jnp.float32
BF16 = jnp.bfloat16
LANES = 128
ROWS = 3
OWN = 2
TOP = 2.0**14


def blocks():
    return [(k, j) for k in range(ROWS) for j in range(ROWS - 1)] + [
        (k, ROWS - 1) for k in range(ROWS)
    ]


def wide(row):
    return jnp.transpose(jnp.broadcast_to(row, (row.shape[1], row.shape[1])))


def spread(tile, width):
    whole = [tile] * (width // LANES)
    rest = [tile[:, : width % LANES]] if width % LANES else []
    return jnp.concatenate(whole + rest, axis=1)


def norm_rows(value, gain):
    mean = jnp.mean(value, axis=0, keepdims=True)
    cent = value - mean
    var = jnp.mean(cent * cent, axis=0, keepdims=True)
    return (cent * lax.rsqrt(var + 1e-05) * spread(gain, value.shape[1])).astype(BF16)


def mix(weight, value):
    return lax.dot_general(weight, value, (((0,), (0,)), ((), ())), preferred_element_type=F32)


def sigmoid(value):
    return 0.5 * jnp.tanh(0.5 * value) + 0.5


def lane_tiles(value):
    return [value[:, k : k + LANES] for k in range(0, value.shape[1], LANES)]


def put(ref, tile, chan, value):
    parts = value.shape[0]
    ref[pl.ds(tile * OWN + chan, parts, stride=ref.shape[0] // parts), :] = value


def take(ref, tile, chan, parts):
    return ref[pl.ds(tile * OWN + chan, parts, stride=ref.shape[0] // parts), :]


def put_edges(both, proj):
    hidden = proj[0].shape[0] // 2
    parts = hidden // OWN
    left, right = (lane_tiles(sigmoid(p[:hidden]) * p[hidden:]) for p in proj)
    middle = jnp.concatenate([left[-1], right[-1]], axis=1)
    for k, tile in enumerate([*left[:-1], middle, *right[:-1]]):
        for chan in range(OWN):
            put(both, k, chan, tile[chan * parts : (chan + 1) * parts])


def first_kernel(
    pair,
    norm_in,
    w_proj,
    w_gate,
    norm_mid,
    w_out,
    both,
    normed,
    state,
    norm_in_near,
    w_proj_near,
    w_gate_near,
    norm_mid_near,
    w_out_near,
    pair_near,
    sems,
):
    cols, chans = pair.shape[1:]
    half = cols // 2
    parts = cols // ROWS
    ends = [(norm_in, norm_in_near)]
    for k in range(ROWS):
        for h in (0, half):
            ends.append((pair.at[k, pl.ds(h, half)], pair_near.at[k, pl.ds(h, half)]))
    ends += [
        (w_proj.at[0], w_proj_near.at[0]),
        (w_gate, w_gate_near),
        (w_proj.at[1], w_proj_near.at[1]),
        (norm_mid, norm_mid_near),
        (w_out, w_out_near),
    ]
    moves = [pltpu.make_async_copy(*pair_of, sems.at[k]) for k, pair_of in enumerate(ends)]
    for move in moves:
        move.start()
    for move in moves[:7]:
        move.wait()
    value = jnp.transpose(
        jnp.concatenate(
            [pair_near[k, pl.ds(j, parts, stride=ROWS), :] for k, j in blocks()], axis=0
        )
    )
    state[...] = value
    gain = wide(norm_in_near[0:1, :])
    moves[7].wait()
    normed[...] = norm_rows(value, gain)
    proj = mix(w_proj_near[0], normed[...])
    put_edges(both, (proj[: 2 * chans], proj[2 * chans :]))
    for move in moves[8:]:
        move.wait()


def middle_kernel(got, state, gate, w_proj, gains, units, w_out, both, normed, state_next):
    chans, places = state.shape
    parts = chans // OWN
    tri = [
        jnp.concatenate([take(got, k, chan, parts) for chan in range(OWN)], axis=0)
        for k in range(pl.cdiv(places, LANES))
    ]
    tri = jnp.concatenate([tile * units[0] for tile in tri], axis=1)[:, :places]
    value = state[...] + gate[...] * mix(w_out[0], norm_rows(tri, gains[0]))
    state_next[...] = value
    normed[...] = norm_rows(value, gains[2])
    each = w_proj.shape[2] // 2
    put_edges(both, [mix(w_proj[1][:, k : k + each], normed[...]) for k in (0, each)])


def last_kernel(got, state, gate, gains, units, w_out, out, near, sems):
    cols, chans = out.shape[1:]
    parts = cols // ROWS
    order = blocks()
    moves = []
    for tiles, rows in (((0, 1, 3), (0, 1)), ((2, 4), (2,))):
        mine = [n for n in range(len(order)) if n // 2 in tiles]
        width = len(mine) * parts

        def lanes(ref):
            pieces = [ref[:, k * LANES : min((k + 1) * LANES, ref.shape[1])] for k in tiles]
            return jnp.concatenate(pieces, axis=1)

        tri = [
            jnp.concatenate([take(got, k, chan, parts) for chan in range(OWN)], axis=0)
            for k in tiles
        ]
        tri = jnp.concatenate([tile * units[1] for tile in tri], axis=1)[:, :width]
        value = lanes(state) + lanes(gate) * mix(w_out[1], norm_rows(tri, gains[1]))
        turned = jnp.transpose(value)
        for place, n in enumerate(mine):
            row, slot = order[n]
            near[row, pl.ds(slot, parts, stride=ROWS), :] = turned[
                place * parts : (place + 1) * parts
            ]
        block = pl.ds(rows[0], len(rows))
        move = pltpu.make_async_copy(near.at[block], out.at[block], sems.at[len(moves)])
        move.start()
        moves.append(move)
    for move in moves:
        move.wait()


def square(mains, tail, last):
    half = LANES // 2
    tails = [tail[:, :half], tail[:, half:], last]
    rows = [jnp.concatenate([main, end], axis=1) for main, end in zip(mains, tails)]
    return jnp.concatenate(rows, axis=0).astype(BF16)


def product(got, scales, out, dims):
    parts = scales.shape[0] // OWN
    half = LANES // 2
    me = lax.axis_index("dap")
    for chan in range(OWN):
        tiles = [take(got, k, chan, parts) for k in range(9)]
        left = square(tiles[:3], tiles[3], tiles[4][:, :half])
        right = square(tiles[5:8], tiles[8], tiles[4][:, half:])
        tri = lax.dot_general(left, right, (dims, ((), ())), preferred_element_type=F32)
        tri = [tri[k : k + parts] for k in range(0, tri.shape[0], parts)]
        ends = [row[:, LANES:] for row in tri] + [jnp.zeros((parts, half), F32)]
        tiles = [row[:, :LANES] for row in tri]
        tiles += [jnp.concatenate(ends[k : k + 2], axis=1) for k in (0, 2)]
        scale = scales[pl.ds(chan * parts + me, 1), :]
        for k, tile in enumerate(tiles):
            put(out, k, chan, tile * scale)


def largest(gain, w_proj, cols):
    hidden = w_proj.shape[1] // 4
    weighted = [gain * w_proj[:, k : k + hidden].astype(F32) for k in (hidden, 3 * hidden)]
    left, right = (jnp.sum(w * w, axis=0, keepdims=True) for w in weighted)
    return 1.02 * cols * hidden * jnp.sqrt(left * right) + 1e-20


def outgoing_kernel(
    got, normed, norm_in, w_proj, w_gate, norm_mid, out, gate, gains, units, scales
):
    cols = scales.shape[1] // OWN * ROWS
    for which in range(2):
        gain = wide(norm_in[which : which + 1, :])
        bound = largest(gain, w_proj[which], cols)
        scales[which] = wide(TOP / bound)
        units[which] = wide(bound * (1 / TOP))
        gains[which] = wide(norm_mid[which : which + 1, :])
    gains[2] = gain
    product(got, scales.at[0], out, ((1,), (1,)))
    gate[...] = sigmoid(mix(w_gate[0], normed[...]))


def incoming_kernel(got, normed, w_gate, scales, out, gate):
    product(got, scales.at[1], out, ((0,), (0,)))
    gate[...] = sigmoid(mix(w_gate[1], normed[...]))


def per_device(pair, norm_in, w_proj, w_gate, norm_mid, w_out):
    cols, chans = pair.shape[1:]
    parts = cols // ROWS
    places = ROWS * cols
    tiles = pl.cdiv(places, LANES)
    both_t = jax.ShapeDtypeStruct((parts * OWN * 2 * places // LANES, LANES), F32)
    tri_t = jax.ShapeDtypeStruct((parts * OWN * tiles, LANES), F32)
    flat_t = jax.ShapeDtypeStruct((chans, places), F32)
    normed_t = jax.ShapeDtypeStruct((chans, places), BF16)
    near = pl.BlockSpec(memory_space=pltpu.VMEM)
    far = pl.BlockSpec(memory_space=pl.ANY)
    dma = pltpu.SemaphoreType.DMA

    def call(kernel, ins, outs, scratch=(), in_spec=near, out_spec=near):
        return pl.pallas_call(
            kernel,
            in_specs=[in_spec] * len(ins),
            out_specs=[out_spec] * len(outs),
            out_shape=outs,
            scratch_shapes=scratch,
            compiler_params=pltpu.CompilerParams(vmem_limit_bytes=32 * 2**20),
        )(*ins)

    def exchange(value, kind):
        sent = value.astype(kind).reshape(parts, -1, OWN, LANES)
        got = lax.all_to_all(sent, "dap", 0, 0, tiled=True)
        return got.reshape(value.shape).astype(F32)

    def like(array):
        return jax.ShapeDtypeStruct(array.shape, array.dtype)

    def squares(count):
        return jax.ShapeDtypeStruct((count, chans, chans), F32)

    params = (norm_in, w_proj, w_gate, norm_mid, w_out)
    both, normed, state, norm_in, w_proj, w_gate, norm_mid, w_out = call(
        first_kernel,
        tuple(pltpu.with_memory_space_constraint(a, pltpu.HBM) for a in (pair, *params)),
        [both_t, normed_t, flat_t, *map(like, params)],
        [pltpu.VMEM(pair.shape, F32), dma((12,))],
        in_spec=far,
    )
    tri, gate, gains, units, scales = call(
        outgoing_kernel,
        (exchange(both, BF16), normed, norm_in, w_proj, w_gate, norm_mid),
        [tri_t, flat_t, squares(3), squares(2), squares(2)],
    )
    both, normed, state = call(
        middle_kernel,
        (exchange(tri, jnp.float16), state, gate, w_proj, gains, units, w_out),
        [both_t, normed_t, flat_t],
    )
    tri, gate = call(
        incoming_kernel, (exchange(both, BF16), normed, w_gate, scales), [tri_t, flat_t]
    )
    (out,) = call(
        last_kernel,
        (exchange(tri, jnp.float16), state, gate, gains, units, w_out),
        [like(pair)],
        [pltpu.VMEM(pair.shape, F32), dma((2,))],
        out_spec=far,
    )
    return out


def solution(mesh):
    return jax.shard_map(
        per_device,
        mesh=mesh,
        in_specs=(P(("crop", "dap"), None, None), P(), P(), P(), P(), P()),
        out_specs=P(("crop", "dap"), None, None),
        check_vma=False,
    )
```

```python
import jax
import jax.numpy as jnp
from jax import lax
from jax.experimental import pallas as pl
from jax.experimental.pallas import tpu as pltpu
from jax.sharding import Mesh
from jax.sharding import PartitionSpec as P

F32 = jnp.float32
BF16 = jnp.bfloat16
LANES = 128
ROWS = 3
OWN = 4
CORES = 2
TOP = 2.0**14


def blocks():
    return [(k, j) for k in range(ROWS) for j in range(ROWS - 1)] + [
        (k, ROWS - 1) for k in range(ROWS)
    ]


def wide(row):
    return jnp.transpose(jnp.broadcast_to(row, (row.shape[1], row.shape[1])))


def spread(tile, width):
    whole = [tile] * (width // LANES)
    rest = [tile[:, : width % LANES]] if width % LANES else []
    return jnp.concatenate(whole + rest, axis=1)


def norm_rows(value, gain):
    mean = jnp.mean(value, axis=0, keepdims=True)
    cent = value - mean
    var = jnp.mean(cent * cent, axis=0, keepdims=True)
    return (cent * lax.rsqrt(var + 1e-05) * spread(gain, value.shape[1])).astype(BF16)


def mix(weight, value):
    return lax.dot_general(weight, value, (((0,), (0,)), ((), ())), preferred_element_type=F32)


def sigmoid(value):
    return 0.5 * jnp.tanh(0.5 * value) + 0.5


def lane_tiles(value):
    return [value[:, k : k + LANES] for k in range(0, value.shape[1], LANES)]


def put(ref, row, value):
    ref[pl.ds(row, value.shape[0], stride=ref.shape[0] // value.shape[0]), :] = value


def take(ref, row, parts):
    return ref[pl.ds(row, parts, stride=ref.shape[0] // parts), :]


def put_tiles(ref, tiles, first):
    for k in range(len(tiles[0]) - 1):
        for chan in range(OWN):
            put(ref, first + k * OWN + chan, tiles[chan][k])
    for pair in range(OWN // 2):
        halves = [tiles[2 * pair + k][-1] for k in range(2)]
        row = first + (len(tiles[0]) - 1) * OWN + pair
        put(ref, row, jnp.concatenate(halves, axis=1))


def take_tiles(ref, first, chan, parts):
    tiles = [take(ref, first + k * OWN + chan, parts) for k in range(4)]
    last = take(ref, first + 4 * OWN + chan // 2, parts)
    start = chan % 2 * (LANES // 2)
    return tiles + [last[:, start : start + LANES // 2]]


def take_rows(ref, tiles, parts):
    mine = [take_tiles(ref, 0, chan, parts) for chan in range(OWN)]
    return [jnp.concatenate([m[k] for m in mine], axis=0) for k in tiles]


def put_edges(both, proj):
    hidden = proj[0].shape[0] // 2
    parts = hidden // OWN
    for side, p in enumerate(proj):
        edge = sigmoid(p[:hidden]) * p[hidden:]
        tiles = [lane_tiles(edge[k : k + parts]) for k in range(0, hidden, parts)]
        put_tiles(both, tiles, side * 18)


def first_kernel(
    pair,
    norm_in,
    w_proj,
    w_gate,
    norm_mid,
    w_out,
    both,
    normed,
    state,
    norm_in_near,
    w_proj_near,
    w_gate_near,
    norm_mid_near,
    w_out_near,
    pair_near,
    sems,
):
    cols, chans = pair.shape[1:]
    half = cols // 2
    parts = cols // (ROWS * CORES)
    ends = [(norm_in, norm_in_near)]
    for k in range(ROWS):
        for h in (0, half):
            ends.append((pair.at[k, pl.ds(h, half)], pair_near.at[k, pl.ds(h, half)]))
    ends += [
        (w_proj.at[0], w_proj_near.at[0]),
        (w_gate, w_gate_near),
        (w_proj.at[1], w_proj_near.at[1]),
        (norm_mid, norm_mid_near),
        (w_out, w_out_near),
    ]
    moves = [pltpu.make_async_copy(*pair_of, sems.at[k]) for k, pair_of in enumerate(ends)]
    for move in moves:
        move.start()
    for move in moves[:7]:
        move.wait()
    value = jnp.transpose(
        jnp.concatenate(
            [
                pair_near[k, pl.ds(core * ROWS + j, parts, stride=CORES * ROWS), :]
                for k, j in blocks()
                for core in range(CORES)
            ],
            axis=0,
        )
    )
    state[...] = value
    gain = wide(norm_in_near[0:1, :])
    moves[7].wait()
    normed[...] = norm_rows(value, gain)
    proj = mix(w_proj_near[0], normed[...])
    put_edges(both, (proj[: 2 * chans], proj[2 * chans :]))
    for move in moves[8:]:
        move.wait()


def middle_kernel(got, state, gate, w_proj, gains, units, w_out, both, normed, state_next):
    chans, places = state.shape
    parts = chans // OWN
    tri = take_rows(got, range(5), parts)
    tri = jnp.concatenate(tri, axis=1) * spread(units[0], places)
    value = state[...] + gate[...] * mix(w_out[0], norm_rows(tri, gains[0]))
    state_next[...] = value
    normed[...] = norm_rows(value, gains[2])
    each = w_proj.shape[2] // 2
    put_edges(both, [mix(w_proj[1][:, k : k + each], normed[...]) for k in (0, each)])


def last_kernel(got, state, gate, gains, units, w_out, out, near, sems):
    cols, chans = out.shape[1:]
    parts = cols // (ROWS * CORES)
    order = [(k, core * ROWS + j) for k, j in blocks() for core in range(CORES)]
    moves = []
    for tiles, rows in (((0, 1, 3), (0, 1)), ((2, 4), (2,))):
        mine = [n for n in range(len(order)) if n // (2 * CORES) in tiles]
        width = len(mine) * parts

        def lanes(ref):
            pieces = [ref[:, k * LANES : min((k + 1) * LANES, ref.shape[1])] for k in tiles]
            return jnp.concatenate(pieces, axis=1)

        tri = jnp.concatenate(take_rows(got, tiles, parts), axis=1) * spread(units[1], width)
        value = lanes(state) + lanes(gate) * mix(w_out[1], norm_rows(tri, gains[1]))
        turned = jnp.transpose(value)
        for place, n in enumerate(mine):
            row, slot = order[n]
            near[row, pl.ds(slot, parts, stride=CORES * ROWS), :] = turned[
                place * parts : (place + 1) * parts
            ]
        block = pl.ds(rows[0], len(rows))
        move = pltpu.make_async_copy(near.at[block], out.at[block], sems.at[len(moves)])
        move.start()
        moves.append(move)
    for move in moves:
        move.wait()


def square(tiles):
    half = LANES // 2
    tails = [tiles[3][:, :half], tiles[3][:, half:], tiles[4]]
    return [jnp.concatenate([main, end], axis=1) for main, end in zip(tiles[:3], tails)]


def stack(rows):
    return jnp.concatenate(rows, axis=0).astype(BF16)


def product_tiles(rows, scale):
    tails = [row[:, LANES:] for row in rows]
    tiles = [row[:, :LANES] * scale for row in rows]
    tiles.append(jnp.concatenate(tails[:2], axis=1) * scale)
    return tiles + [tails[2] * scale[:, : LANES // 2]]


def scale_of(scales, chan):
    parts = scales.shape[0] // OWN
    return scales[pl.ds(chan * parts + lax.axis_index("chip"), 1), :]


def largest(gain, w_proj, cols):
    hidden = w_proj.shape[1] // 4
    weighted = [gain * w_proj[:, k : k + hidden].astype(F32) for k in (hidden, 3 * hidden)]
    left, right = (jnp.sum(w * w, axis=0, keepdims=True) for w in weighted)
    return 1.02 * cols * hidden * jnp.sqrt(left * right) + 1e-20


def outgoing_kernel(
    got, other, normed, norm_in, w_proj, w_gate, norm_mid, out, gate, gains, units, scales
):
    parts = scales.shape[1] // OWN
    for which in range(2):
        gain = wide(norm_in[which : which + 1, :])
        bound = largest(gain, w_proj[which], parts * CORES * ROWS)
        scales[which] = wide(TOP / bound)
        units[which] = wide(bound * (1 / TOP))
        gains[which] = wide(norm_mid[which : which + 1, :])
    gains[2] = gain
    first = lax.axis_index("core") == 0
    tiles = []
    for chan in range(OWN):
        left = stack(square(take_tiles(got, 0, chan, parts)))
        own = square(take_tiles(got, 18, chan, parts))
        far = square(take_tiles(other, 0, chan, parts))
        right = []
        for mine, theirs in zip(own, far):
            right += [jnp.where(first, mine, theirs), jnp.where(first, theirs, mine)]
        tri = lax.dot_general(
            left, stack(right), (((1,), (1,)), ((), ())), preferred_element_type=F32
        )
        rows = [tri[k : k + parts] for k in range(0, tri.shape[0], parts)]
        tiles.append(product_tiles(rows, scale_of(scales.at[0], chan)))
    put_tiles(out, tiles, 0)
    gate[...] = sigmoid(mix(w_gate[0], normed[...]))


def incoming_kernel(got, normed, w_gate, scales, out, out_other, gate):
    parts = scales.shape[1] // OWN
    first = lax.axis_index("core") == 0
    kept, given = [], []
    for chan in range(OWN):
        left = stack(square(take_tiles(got, 0, chan, parts)))
        right = stack(square(take_tiles(got, 18, chan, parts)))
        tri = mix(left, right)
        rows = [tri[k : k + parts] for k in range(0, tri.shape[0], parts)]
        pairs = list(zip(rows[0::2], rows[1::2]))
        scale = scale_of(scales.at[1], chan)
        kept.append(product_tiles([jnp.where(first, a, b) for a, b in pairs], scale))
        given.append(product_tiles([jnp.where(first, b, a) for a, b in pairs], scale))
    put_tiles(out, kept, 0)
    put_tiles(out_other, given, 0)
    gate[...] = sigmoid(mix(w_gate[1], normed[...]))


def per_device(pair, norm_in, w_proj, w_gate, norm_mid, w_out):
    cols, chans = pair.shape[1:]
    parts = cols // (ROWS * CORES)
    places = ROWS * cols
    tri_t = jax.ShapeDtypeStruct((parts * OWN * places // LANES, LANES), F32)
    both_t = jax.ShapeDtypeStruct((2 * tri_t.shape[0], LANES), F32)
    flat_t = jax.ShapeDtypeStruct((chans, places), F32)
    normed_t = jax.ShapeDtypeStruct((chans, places), BF16)
    near = pl.BlockSpec(memory_space=pltpu.VMEM)
    far = pl.BlockSpec(memory_space=pl.ANY)
    dma = pltpu.SemaphoreType.DMA

    def call(kernel, ins, outs, scratch=(), in_spec=near, out_spec=near):
        return pl.pallas_call(
            kernel,
            in_specs=[in_spec] * len(ins),
            out_specs=[out_spec] * len(outs),
            out_shape=outs,
            scratch_shapes=scratch,
            compiler_params=pltpu.CompilerParams(vmem_limit_bytes=32 * 2**20),
        )(*ins)

    def exchange(value):
        sent = value.reshape(parts, -1, 2, LANES)
        return lax.all_to_all(sent, "chip", 0, 0, tiled=True)

    def swap(value):
        return lax.ppermute(value, "core", [(0, 1), (1, 0)])

    def rows_of(value):
        return value.reshape(-1, LANES).astype(F32)

    def like(array):
        return jax.ShapeDtypeStruct(array.shape, array.dtype)

    def squares(count):
        return jax.ShapeDtypeStruct((count, chans, chans), F32)

    params = (norm_in, w_proj, w_gate, norm_mid, w_out)
    both, normed, state, norm_in, w_proj, w_gate, norm_mid, w_out = call(
        first_kernel,
        tuple(pltpu.with_memory_space_constraint(a, pltpu.HBM) for a in (pair, *params)),
        [both_t, normed_t, flat_t, *map(like, params)],
        [pltpu.VMEM(pair.shape, F32), dma((12,))],
        in_spec=far,
    )
    got = exchange(both.astype(BF16))
    other = swap(got[:, got.shape[1] // 2 :])
    tri, gate, gains, units, scales = call(
        outgoing_kernel,
        (rows_of(got), rows_of(other), normed, norm_in, w_proj, w_gate, norm_mid),
        [tri_t, flat_t, squares(3), squares(2), squares(2)],
    )
    got = exchange(tri.astype(jnp.float16))
    both, normed, state = call(
        middle_kernel,
        (rows_of(got), state, gate, w_proj, gains, units, w_out),
        [both_t, normed_t, flat_t],
    )
    got = exchange(both.astype(BF16))
    tri, given, gate = call(
        incoming_kernel, (rows_of(got), normed, w_gate, scales), [tri_t, tri_t, flat_t]
    )
    tri = tri + swap(given.astype(jnp.float16)).astype(F32)
    got = exchange(tri.astype(jnp.float16))
    (out,) = call(
        last_kernel,
        (rows_of(got), state, gate, gains, units, w_out),
        [like(pair)],
        [pltpu.VMEM(pair.shape, F32), dma((2,))],
        out_spec=far,
    )
    return out


def solution(mesh):
    crops, devices = mesh.devices.shape
    split = Mesh(mesh.devices.reshape(crops, devices // CORES, CORES), ("crop", "chip", "core"))
    whole = P(("crop", "chip", "core"), None, None)
    return jax.shard_map(
        per_device,
        mesh=split,
        in_specs=(whole, P(), P(), P(), P(), P()),
        out_specs=whole,
        check_vma=False,
    )
```

```python
import jax
import jax.numpy as jnp
from jax import lax
from jax.experimental import pallas as pl
from jax.experimental.pallas import tpu as pltpu
from jax.sharding import Mesh
from jax.sharding import PartitionSpec as P

F32 = jnp.float32
BF16 = jnp.bfloat16
LANES = 128
ROWS = 3
OWN = 4
CORES = 2
TOP = 2.0**14


def blocks():
    return [(k, j) for k in range(ROWS) for j in range(ROWS - 1)] + [
        (k, ROWS - 1) for k in range(ROWS)
    ]


def wide(row):
    return jnp.transpose(jnp.broadcast_to(row, (row.shape[1], row.shape[1])))


def spread(tile, width):
    whole = [tile] * (width // LANES)
    rest = [tile[:, : width % LANES]] if width % LANES else []
    return jnp.concatenate(whole + rest, axis=1)


def norm_rows(value, gain):
    mean = jnp.mean(value, axis=0, keepdims=True)
    cent = value - mean
    var = jnp.mean(cent * cent, axis=0, keepdims=True)
    return (cent * lax.rsqrt(var + 1e-05) * spread(gain, value.shape[1])).astype(BF16)


def mix(weight, value):
    return lax.dot_general(weight, value, (((0,), (0,)), ((), ())), preferred_element_type=F32)


def sigmoid(value):
    return 0.5 * jnp.tanh(0.5 * value) + 0.5


def lane_tiles(value):
    return [value[:, k : k + LANES] for k in range(0, value.shape[1], LANES)]


def put(ref, row, value):
    ref[pl.ds(row, value.shape[0], stride=ref.shape[0] // value.shape[0]), :] = value


def take(ref, row, parts):
    return ref[pl.ds(row, parts, stride=ref.shape[0] // parts), :]


def put_tiles(ref, tiles, first):
    for k in range(len(tiles[0]) - 1):
        for chan in range(OWN):
            put(ref, first + k * OWN + chan, tiles[chan][k])
    for pair in range(OWN // 2):
        halves = [tiles[2 * pair + k][-1] for k in range(2)]
        row = first + (len(tiles[0]) - 1) * OWN + pair
        put(ref, row, jnp.concatenate(halves, axis=1))


def take_tiles(ref, first, chan, parts):
    tiles = [take(ref, first + k * OWN + chan, parts) for k in range(4)]
    last = take(ref, first + 4 * OWN + chan // 2, parts)
    start = chan % 2 * (LANES // 2)
    return tiles + [last[:, start : start + LANES // 2]]


def take_rows(ref, tiles, parts):
    mine = [take_tiles(ref, 0, chan, parts) for chan in range(OWN)]
    return [jnp.concatenate([m[k] for m in mine], axis=0) for k in tiles]


def put_edges(both, proj):
    hidden = proj[0].shape[0] // 2
    parts = hidden // OWN
    for side, p in enumerate(proj):
        edge = sigmoid(p[:hidden]) * p[hidden:]
        tiles = [lane_tiles(edge[k : k + parts]) for k in range(0, hidden, parts)]
        put_tiles(both, tiles, side * 18)


def first_kernel(
    pair,
    norm_in,
    w_proj,
    w_gate,
    norm_mid,
    w_out,
    both,
    normed,
    state,
    norm_in_near,
    w_proj_near,
    w_gate_near,
    norm_mid_near,
    w_out_near,
    pair_near,
    sems,
):
    cols, chans = pair.shape[1:]
    half = cols // 2
    parts = cols // (ROWS * CORES)
    ends = [(norm_in, norm_in_near)]
    for k in range(ROWS):
        for h in (0, half):
            ends.append((pair.at[k, pl.ds(h, half)], pair_near.at[k, pl.ds(h, half)]))
    ends += [
        (w_proj.at[0], w_proj_near.at[0]),
        (w_gate, w_gate_near),
        (w_proj.at[1], w_proj_near.at[1]),
        (norm_mid, norm_mid_near),
        (w_out, w_out_near),
    ]
    moves = [pltpu.make_async_copy(*pair_of, sems.at[k]) for k, pair_of in enumerate(ends)]
    for move in moves:
        move.start()
    for move in moves[:7]:
        move.wait()
    value = jnp.transpose(
        jnp.concatenate(
            [
                pair_near[k, pl.ds(core * ROWS + j, parts, stride=CORES * ROWS), :]
                for k, j in blocks()
                for core in range(CORES)
            ],
            axis=0,
        )
    )
    state[...] = value
    gain = wide(norm_in_near[0:1, :])
    moves[7].wait()
    normed[...] = norm_rows(value, gain)
    proj = mix(w_proj_near[0], normed[...])
    put_edges(both, (proj[: 2 * chans], proj[2 * chans :]))
    for move in moves[8:]:
        move.wait()


def middle_kernel(got, state, gate, w_proj, gains, units, w_out, both, normed, state_next):
    chans, places = state.shape
    parts = chans // OWN
    tri = take_rows(got, range(5), parts)
    tri = jnp.concatenate(tri, axis=1) * spread(units[0], places)
    value = state[...] + gate[...] * mix(w_out[0], norm_rows(tri, gains[0]))
    state_next[...] = value
    ready = norm_rows(value, gains[2])
    normed[...] = ready
    each = w_proj.shape[2] // 2
    proj = mix(w_proj[1], ready)
    put_edges(both, (proj[:each], proj[each:]))


def last_kernel(got, state, gate, gains, units, w_out, out, near, sems):
    cols, chans = out.shape[1:]
    parts = cols // (ROWS * CORES)
    order = [(k, core * ROWS + j) for k, j in blocks() for core in range(CORES)]
    moves = []
    for tiles, rows in (((0, 1, 3), (0, 1)), ((2, 4), (2,))):
        mine = [n for n in range(len(order)) if n // (2 * CORES) in tiles]
        width = len(mine) * parts

        def lanes(ref):
            pieces = [ref[:, k * LANES : min((k + 1) * LANES, ref.shape[1])] for k in tiles]
            return jnp.concatenate(pieces, axis=1)

        tri = jnp.concatenate(take_rows(got, tiles, parts), axis=1) * spread(units[1], width)
        value = lanes(state) + lanes(gate) * mix(w_out[1], norm_rows(tri, gains[1]))
        turned = jnp.transpose(value)
        for place, n in enumerate(mine):
            row, slot = order[n]
            near[row, pl.ds(slot, parts, stride=CORES * ROWS), :] = turned[
                place * parts : (place + 1) * parts
            ]
        block = pl.ds(rows[0], len(rows))
        move = pltpu.make_async_copy(near.at[block], out.at[block], sems.at[len(moves)])
        move.start()
        moves.append(move)
    for move in moves:
        move.wait()


def square(tiles):
    half = LANES // 2
    tails = [tiles[3][:, :half], tiles[3][:, half:], tiles[4]]
    return [jnp.concatenate([main, end], axis=1) for main, end in zip(tiles[:3], tails)]


def stack(rows):
    return jnp.concatenate(rows, axis=0).astype(BF16)


def product_tiles(rows, scale):
    tails = [row[:, LANES:] for row in rows]
    tiles = [row[:, :LANES] * scale for row in rows]
    tiles.append(jnp.concatenate(tails[:2], axis=1) * scale)
    return tiles + [tails[2] * scale[:, : LANES // 2]]


def scale_of(scales, chan):
    parts = scales.shape[0] // OWN
    return scales[pl.ds(chan * parts + lax.axis_index("chip"), 1), :]


def largest(gain, w_proj, cols):
    hidden = w_proj.shape[1] // 4
    weighted = [gain * w_proj[:, k : k + hidden].astype(F32) for k in (hidden, 3 * hidden)]
    left, right = (jnp.sum(w * w, axis=0, keepdims=True) for w in weighted)
    return 1.02 * cols * hidden * jnp.sqrt(left * right) + 1e-20


def prepare_kernel(
    got, normed, norm_in, w_proj, w_gate, norm_mid, left, own, gate, gains, units, scales
):
    parts = scales.shape[1] // OWN
    for which in range(2):
        gain = wide(norm_in[which : which + 1, :])
        bound = largest(gain, w_proj[which], parts * CORES * ROWS)
        scales[which] = wide(TOP / bound)
        units[which] = wide(bound * (1 / TOP))
        gains[which] = wide(norm_mid[which : which + 1, :])
    gains[2] = gain
    for chan in range(OWN):
        left[chan] = stack(square(take_tiles(got, 0, chan, parts)))
        own[chan] = stack(square(take_tiles(got, 18, chan, parts)))
    gate[...] = sigmoid(mix(w_gate[0], normed[...]))


def outgoing_kernel(left, own, other, scales, out):
    parts = scales.shape[1] // OWN
    first = lax.axis_index("core") == 0
    tiles = []
    for chan in range(OWN):
        far = stack(square(take_tiles(other, 0, chan, parts)))
        right = []
        for k in range(0, far.shape[0], parts):
            mine, theirs = own[chan, k : k + parts], far[k : k + parts]
            right += [jnp.where(first, mine, theirs), jnp.where(first, theirs, mine)]
        tri = lax.dot_general(
            left[chan],
            jnp.concatenate(right, axis=0),
            (((1,), (1,)), ((), ())),
            preferred_element_type=F32,
        )
        rows = [tri[k : k + parts] for k in range(0, tri.shape[0], parts)]
        tiles.append(product_tiles(rows, scale_of(scales.at[0], chan)))
    put_tiles(out, tiles, 0)


def half_sums(got, scales, out, core):
    parts = scales.shape[1] // OWN
    first = core == 0
    tiles, sums = [], []
    for chan in range(OWN):
        left = stack(square(take_tiles(got, 0, chan, parts)))
        right = stack(square(take_tiles(got, 18, chan, parts)))
        turned = jnp.transpose(left)
        rows = [turned[k : k + parts] for k in range(0, turned.shape[0], parts)]
        rows = [jnp.where(first, a, b) for a, b in zip(rows[0::2], rows[1::2])]
        sums.append(
            jnp.dot(jnp.concatenate(rows, axis=0), right, preferred_element_type=F32)
        )
    for chan, tri in enumerate(sums):
        rows = [tri[k : k + parts] for k in range(0, tri.shape[0], parts)]
        tiles.append(product_tiles(rows, scale_of(scales.at[1], chan)))
    put_tiles(out, tiles, 0)


def given_kernel(got, scales, out):
    half_sums(got, scales, out, 1 - lax.axis_index("core"))


def kept_kernel(got, scales, normed, w_gate, out, gate):
    half_sums(got, scales, out, lax.axis_index("core"))
    gate[...] = sigmoid(mix(w_gate[1], normed[...]))


def per_device(pair, norm_in, w_proj, w_gate, norm_mid, w_out):
    cols, chans = pair.shape[1:]
    parts = cols // (ROWS * CORES)
    places = ROWS * cols
    tri_t = jax.ShapeDtypeStruct((parts * OWN * places // LANES, LANES), F32)
    both_t = jax.ShapeDtypeStruct((2 * tri_t.shape[0], LANES), F32)
    flat_t = jax.ShapeDtypeStruct((chans, places), F32)
    normed_t = jax.ShapeDtypeStruct((chans, places), BF16)
    near = pl.BlockSpec(memory_space=pltpu.VMEM)
    far = pl.BlockSpec(memory_space=pl.ANY)
    dma = pltpu.SemaphoreType.DMA

    def call(kernel, ins, outs, scratch=(), in_spec=near, out_spec=near):
        return pl.pallas_call(
            kernel,
            in_specs=[in_spec] * len(ins),
            out_specs=[out_spec] * len(outs),
            out_shape=outs,
            scratch_shapes=scratch,
            compiler_params=pltpu.CompilerParams(vmem_limit_bytes=32 * 2**20),
        )(*ins)

    def exchange(value):
        sent = value.reshape(parts, -1, 2, LANES)
        return lax.all_to_all(sent, "chip", 0, 0, tiled=True)

    def swap(value):
        return lax.ppermute(value, "core", [(0, 1), (1, 0)])

    def rows_of(value):
        return value.reshape(-1, LANES).astype(F32)

    def like(array):
        return jax.ShapeDtypeStruct(array.shape, array.dtype)

    def squares(count):
        return jax.ShapeDtypeStruct((count, chans, chans), F32)

    params = (norm_in, w_proj, w_gate, norm_mid, w_out)
    both, normed, state, norm_in, w_proj, w_gate, norm_mid, w_out = call(
        first_kernel,
        tuple(pltpu.with_memory_space_constraint(a, pltpu.HBM) for a in (pair, *params)),
        [both_t, normed_t, flat_t, *map(like, params)],
        [pltpu.VMEM(pair.shape, F32), dma((12,))],
        in_spec=far,
    )
    got = exchange(both.astype(BF16))
    other = swap(got[:, got.shape[1] // 2 :])
    got = rows_of(got)
    square_t = jax.ShapeDtypeStruct((OWN, cols // CORES, cols), BF16)
    left, own, gate, gains, units, scales = call(
        prepare_kernel,
        (got, normed, norm_in, w_proj, w_gate, norm_mid),
        [square_t, square_t, flat_t, squares(3), squares(2), squares(2)],
    )
    (tri,) = call(outgoing_kernel, (left, own, rows_of(other), scales), [tri_t])
    got = exchange(tri.astype(jnp.float16))
    both, normed, state = call(
        middle_kernel,
        (rows_of(got), state, gate, w_proj, gains, units, w_out),
        [both_t, normed_t, flat_t],
    )
    got = rows_of(exchange(both.astype(BF16)))
    (given,) = call(given_kernel, (got, scales), [tri_t])
    other = swap(given.astype(jnp.float16))
    tri, gate = call(kept_kernel, (got, scales, normed, w_gate), [tri_t, flat_t])
    tri = tri + other.astype(F32)
    got = exchange(tri.astype(jnp.float16))
    (out,) = call(
        last_kernel,
        (rows_of(got), state, gate, gains, units, w_out),
        [like(pair)],
        [pltpu.VMEM(pair.shape, F32), dma((2,))],
        out_spec=far,
    )
    return out


def solution(mesh):
    crops, devices = mesh.devices.shape
    split = Mesh(mesh.devices.reshape(crops, devices // CORES, CORES), ("crop", "chip", "core"))
    whole = P(("crop", "chip", "core"), None, None)
    return jax.shard_map(
        per_device,
        mesh=split,
        in_specs=(whole, P(), P(), P(), P(), P()),
        out_specs=whole,
        check_vma=False,
    )
```

```python
import jax
import jax.numpy as jnp
from jax import lax
from jax.experimental import pallas as pl
from jax.experimental.pallas import tpu as pltpu
from jax.sharding import Mesh
from jax.sharding import PartitionSpec as P

F32 = jnp.float32
BF16 = jnp.bfloat16
LANES = 128
ROWS = 3
OWN = 4
CORES = 2
TOP = 2.0**14


def blocks():
    return [(k, j) for k in range(ROWS) for j in range(ROWS - 1)] + [
        (k, ROWS - 1) for k in range(ROWS)
    ]


def wide(row):
    return jnp.transpose(jnp.broadcast_to(row, (row.shape[1], row.shape[1])))


def spread(tile, width):
    whole = [tile] * (width // LANES)
    rest = [tile[:, : width % LANES]] if width % LANES else []
    return jnp.concatenate(whole + rest, axis=1)


def norm_rows(value, gain):
    mean = jnp.mean(value, axis=0, keepdims=True)
    cent = value - mean
    var = jnp.mean(cent * cent, axis=0, keepdims=True)
    return (cent * lax.rsqrt(var + 1e-05) * spread(gain, value.shape[1])).astype(BF16)


def mix(weight, value):
    return lax.dot_general(weight, value, (((0,), (0,)), ((), ())), preferred_element_type=F32)


def sigmoid(half):
    return 0.5 * jnp.tanh(half) + 0.5


def lane_tiles(value):
    return [value[:, k : k + LANES] for k in range(0, value.shape[1], LANES)]


def put(ref, row, value):
    ref[pl.ds(row, value.shape[0], stride=ref.shape[0] // value.shape[0]), :] = value


def take(ref, row, parts):
    return ref[pl.ds(row, parts, stride=ref.shape[0] // parts), :]


def put_tiles(ref, tiles, first):
    for k in range(len(tiles[0]) - 1):
        for chan in range(OWN):
            put(ref, first + k * OWN + chan, tiles[chan][k])
    for pair in range(OWN // 2):
        halves = [tiles[2 * pair + k][-1] for k in range(2)]
        row = first + (len(tiles[0]) - 1) * OWN + pair
        put(ref, row, jnp.concatenate(halves, axis=1))


def take_tiles(ref, first, chan, parts):
    tiles = [take(ref, first + k * OWN + chan, parts) for k in range(4)]
    last = take(ref, first + 4 * OWN + chan // 2, parts)
    start = chan % 2 * (LANES // 2)
    return tiles + [last[:, start : start + LANES // 2]]


def take_rows(ref, tiles, parts):
    mine = [take_tiles(ref, 0, chan, parts) for chan in range(OWN)]
    return [jnp.concatenate([m[k] for m in mine], axis=0) for k in tiles]


def put_edges(both, proj):
    hidden = proj[0].shape[0] // 2
    parts = hidden // OWN
    for side, p in enumerate(proj):
        edge = (jnp.tanh(p[:hidden]) + 1.0) * p[hidden:]
        tiles = [lane_tiles(edge[k : k + parts]) for k in range(0, hidden, parts)]
        put_tiles(both, tiles, side * 18)


def first_kernel(
    pair,
    norm_in,
    w_proj,
    w_gate,
    norm_mid,
    w_out,
    both,
    normed,
    state,
    norm_in_near,
    w_proj_near,
    w_gate_near,
    norm_mid_near,
    w_out_near,
    pair_near,
    sems,
):
    cols, chans = pair.shape[1:]
    half = cols // 2
    parts = cols // (ROWS * CORES)
    ends = [(norm_in, norm_in_near)]
    for k in range(ROWS):
        for h in (0, half):
            ends.append((pair.at[k, pl.ds(h, half)], pair_near.at[k, pl.ds(h, half)]))
    ends += [
        (w_proj.at[0], w_proj_near.at[0]),
        (w_gate, w_gate_near),
        (w_proj.at[1], w_proj_near.at[1]),
        (norm_mid, norm_mid_near),
        (w_out, w_out_near),
    ]
    moves = [pltpu.make_async_copy(*pair_of, sems.at[k]) for k, pair_of in enumerate(ends)]
    for move in moves:
        move.start()
    for move in moves[:7]:
        move.wait()
    value = jnp.transpose(
        jnp.concatenate(
            [
                pair_near[k, pl.ds(core * ROWS + j, parts, stride=CORES * ROWS), :]
                for k, j in blocks()
                for core in range(CORES)
            ],
            axis=0,
        )
    )
    state[...] = value
    gain = wide(0.5 * norm_in_near[0:1, :])
    moves[7].wait()
    normed[...] = norm_rows(value, gain)
    proj = mix(w_proj_near[0], normed[...])
    put_edges(both, (proj[: 2 * chans], proj[2 * chans :]))
    for move in moves[8:]:
        move.wait()


def middle_kernel(got, state, gate, w_proj, gains, units, w_out, both, normed, state_next):
    chans, places = state.shape
    parts = chans // OWN
    tri = take_rows(got, range(5), parts)
    tri = jnp.concatenate(tri, axis=1) * spread(units[0], places)
    value = state[...] + gate[...] * mix(w_out[0], norm_rows(tri, gains[0]))
    state_next[...] = value
    ready = norm_rows(value, gains[2])
    normed[...] = ready
    each = w_proj.shape[2] // 2
    proj = mix(w_proj[1], ready)
    put_edges(both, (proj[:each], proj[each:]))


def last_kernel(got, state, gate, gains, units, w_out, out, near, sems):
    cols, chans = out.shape[1:]
    parts = cols // (ROWS * CORES)
    order = [(k, core * ROWS + j) for k, j in blocks() for core in range(CORES)]
    moves = []
    for tiles, rows in (((0, 1, 3), (0, 1)), ((2, 4), (2,))):
        mine = [n for n in range(len(order)) if n // (2 * CORES) in tiles]
        width = len(mine) * parts

        def lanes(ref):
            pieces = [ref[:, k * LANES : min((k + 1) * LANES, ref.shape[1])] for k in tiles]
            return jnp.concatenate(pieces, axis=1)

        tri = jnp.concatenate(take_rows(got, tiles, parts), axis=1) * spread(units[1], width)
        value = lanes(state) + lanes(gate) * mix(w_out[1], norm_rows(tri, gains[1]))
        turned = jnp.transpose(value)
        for place, n in enumerate(mine):
            row, slot = order[n]
            near[row, pl.ds(slot, parts, stride=CORES * ROWS), :] = turned[
                place * parts : (place + 1) * parts
            ]
        block = pl.ds(rows[0], len(rows))
        move = pltpu.make_async_copy(near.at[block], out.at[block], sems.at[len(moves)])
        move.start()
        moves.append(move)
    for move in moves:
        move.wait()


def square(tiles):
    half = LANES // 2
    tails = [tiles[3][:, :half], tiles[3][:, half:], tiles[4]]
    return [jnp.concatenate([main, end], axis=1) for main, end in zip(tiles[:3], tails)]


def stack(rows):
    return jnp.concatenate(rows, axis=0).astype(BF16)


def product_tiles(rows, scale):
    tails = [row[:, LANES:] for row in rows]
    tiles = [row[:, :LANES] * scale for row in rows]
    tiles.append(jnp.concatenate(tails[:2], axis=1) * scale)
    return tiles + [tails[2] * scale[:, : LANES // 2]]


def scale_of(scales, chan):
    parts = scales.shape[0] // OWN
    return scales[pl.ds(chan * parts + lax.axis_index("chip"), 1), :]


def largest(gain, w_proj, cols):
    hidden = w_proj.shape[1] // 4
    weighted = [gain * w_proj[:, k : k + hidden].astype(F32) for k in (hidden, 3 * hidden)]
    left, right = (jnp.sum(w * w, axis=0, keepdims=True) for w in weighted)
    return 1.02 * cols * hidden * jnp.sqrt(left * right) + 1e-20


def prepare_kernel(
    got, normed, norm_in, w_proj, w_gate, norm_mid, left, own, gate, gains, units, scales
):
    parts = scales.shape[1] // OWN
    for which in range(2):
        gain = wide(norm_in[which : which + 1, :])
        bound = largest(gain, w_proj[which], parts * CORES * ROWS)
        scales[which] = wide(TOP / bound)
        units[which] = wide(bound * (1 / TOP))
        gains[which] = wide(norm_mid[which : which + 1, :])
    gains[2] = 0.5 * gain
    for chan in range(OWN):
        left[chan] = stack(square(take_tiles(got, 0, chan, parts)))
        own[chan] = stack(square(take_tiles(got, 18, chan, parts)))
    gate[...] = sigmoid(mix(w_gate[0], normed[...]))


def outgoing_kernel(left, own, other, scales, out):
    parts = scales.shape[1] // OWN
    first = lax.axis_index("core") == 0
    tiles = []
    for chan in range(OWN):
        far = stack(square(take_tiles(other, 0, chan, parts)))
        right = []
        for k in range(0, far.shape[0], parts):
            mine, theirs = own[chan, k : k + parts], far[k : k + parts]
            right += [jnp.where(first, mine, theirs), jnp.where(first, theirs, mine)]
        tri = lax.dot_general(
            left[chan],
            jnp.concatenate(right, axis=0),
            (((1,), (1,)), ((), ())),
            preferred_element_type=F32,
        )
        rows = [tri[k : k + parts] for k in range(0, tri.shape[0], parts)]
        tiles.append(product_tiles(rows, scale_of(scales.at[0], chan)))
    put_tiles(out, tiles, 0)


def half_sums(got, scales, out, core):
    parts = scales.shape[1] // OWN
    first = core == 0
    tiles, sums = [], []
    for chan in range(OWN):
        left = stack(square(take_tiles(got, 0, chan, parts)))
        right = stack(square(take_tiles(got, 18, chan, parts)))
        turned = jnp.transpose(left)
        rows = [turned[k : k + parts] for k in range(0, turned.shape[0], parts)]
        rows = [jnp.where(first, a, b) for a, b in zip(rows[0::2], rows[1::2])]
        sums.append(
            jnp.dot(jnp.concatenate(rows, axis=0), right, preferred_element_type=F32)
        )
    for chan, tri in enumerate(sums):
        rows = [tri[k : k + parts] for k in range(0, tri.shape[0], parts)]
        tiles.append(product_tiles(rows, scale_of(scales.at[1], chan)))
    put_tiles(out, tiles, 0)


def given_kernel(got, scales, out):
    half_sums(got, scales, out, 1 - lax.axis_index("core"))


def kept_kernel(got, scales, normed, w_gate, out, gate):
    half_sums(got, scales, out, lax.axis_index("core"))
    gate[...] = sigmoid(mix(w_gate[1], normed[...]))


def per_device(pair, norm_in, w_proj, w_gate, norm_mid, w_out):
    cols, chans = pair.shape[1:]
    parts = cols // (ROWS * CORES)
    places = ROWS * cols
    tri_t = jax.ShapeDtypeStruct((parts * OWN * places // LANES, LANES), F32)
    both_t = jax.ShapeDtypeStruct((2 * tri_t.shape[0], LANES), F32)
    flat_t = jax.ShapeDtypeStruct((chans, places), F32)
    normed_t = jax.ShapeDtypeStruct((chans, places), BF16)
    near = pl.BlockSpec(memory_space=pltpu.VMEM)
    far = pl.BlockSpec(memory_space=pl.ANY)
    dma = pltpu.SemaphoreType.DMA

    def call(kernel, ins, outs, scratch=(), in_spec=near, out_spec=near):
        return pl.pallas_call(
            kernel,
            in_specs=[in_spec] * len(ins),
            out_specs=[out_spec] * len(outs),
            out_shape=outs,
            scratch_shapes=scratch,
            compiler_params=pltpu.CompilerParams(vmem_limit_bytes=32 * 2**20),
        )(*ins)

    def exchange(value):
        sent = value.reshape(parts, -1, 2, LANES)
        return lax.all_to_all(sent, "chip", 0, 0, tiled=True)

    def swap(value):
        return lax.ppermute(value, "core", [(0, 1), (1, 0)])

    def rows_of(value):
        return value.reshape(-1, LANES).astype(F32)

    def like(array):
        return jax.ShapeDtypeStruct(array.shape, array.dtype)

    def squares(count):
        return jax.ShapeDtypeStruct((count, chans, chans), F32)

    params = (norm_in, w_proj, w_gate, norm_mid, w_out)
    both, normed, state, norm_in, w_proj, w_gate, norm_mid, w_out = call(
        first_kernel,
        tuple(pltpu.with_memory_space_constraint(a, pltpu.HBM) for a in (pair, *params)),
        [both_t, normed_t, flat_t, *map(like, params)],
        [pltpu.VMEM(pair.shape, F32), dma((12,))],
        in_spec=far,
    )
    got = exchange(both.astype(BF16))
    other = swap(got[:, got.shape[1] // 2 :])
    got = rows_of(got)
    square_t = jax.ShapeDtypeStruct((OWN, cols // CORES, cols), BF16)
    left, own, gate, gains, units, scales = call(
        prepare_kernel,
        (got, normed, norm_in, w_proj, w_gate, norm_mid),
        [square_t, square_t, flat_t, squares(3), squares(2), squares(2)],
    )
    (tri,) = call(outgoing_kernel, (left, own, rows_of(other), scales), [tri_t])
    got = exchange(tri.astype(jnp.float16))
    both, normed, state = call(
        middle_kernel,
        (rows_of(got), state, gate, w_proj, gains, units, w_out),
        [both_t, normed_t, flat_t],
    )
    got = rows_of(exchange(both.astype(BF16)))
    (given,) = call(given_kernel, (got, scales), [tri_t])
    other = swap(given.astype(jnp.float16))
    tri, gate = call(kept_kernel, (got, scales, normed, w_gate), [tri_t, flat_t])
    tri = tri + other.astype(F32)
    got = exchange(tri.astype(jnp.float16))
    (out,) = call(
        last_kernel,
        (rows_of(got), state, gate, gains, units, w_out),
        [like(pair)],
        [pltpu.VMEM(pair.shape, F32), dma((2,))],
        out_spec=far,
    )
    return out


def solution(mesh):
    crops, devices = mesh.devices.shape
    split = Mesh(mesh.devices.reshape(crops, devices // CORES, CORES), ("crop", "chip", "core"))
    whole = P(("crop", "chip", "core"), None, None)
    return jax.shard_map(
        per_device,
        mesh=split,
        in_specs=(whole, P(), P(), P(), P(), P()),
        out_specs=whole,
        check_vma=False,
    )
```

```python
import jax
import jax.numpy as jnp
from jax import lax
from jax.experimental import pallas as pl
from jax.experimental.pallas import tpu as pltpu
from jax.sharding import Mesh
from jax.sharding import PartitionSpec as P

F32 = jnp.float32
BF16 = jnp.bfloat16
LANES = 128
ROWS = 3
OWN = 4
CORES = 2
TOP = 2.0**14


def blocks():
    return [(k, j) for k in range(ROWS) for j in range(ROWS - 1)] + [
        (k, ROWS - 1) for k in range(ROWS)
    ]


def wide(row):
    return jnp.transpose(jnp.broadcast_to(row, (row.shape[1], row.shape[1])))


def spread(tile, width):
    whole = [tile] * (width // LANES)
    rest = [tile[:, : width % LANES]] if width % LANES else []
    return jnp.concatenate(whole + rest, axis=1)


def norm_rows(value, gain):
    mean = jnp.mean(value, axis=0, keepdims=True)
    cent = value - mean
    var = jnp.mean(cent * cent, axis=0, keepdims=True)
    return (cent * lax.rsqrt(var + 1e-05) * spread(gain, value.shape[1])).astype(BF16)


def mix(weight, value):
    return lax.dot_general(weight, value, (((0,), (0,)), ((), ())), preferred_element_type=F32)


def sigmoid(value):
    return 0.5 * jnp.tanh(0.5 * value) + 0.5


def lane_tiles(value):
    return [value[:, k : k + LANES] for k in range(0, value.shape[1], LANES)]


def put(ref, row, value):
    ref[pl.ds(row, value.shape[0], stride=ref.shape[0] // value.shape[0]), :] = value


def take(ref, row, parts):
    return ref[pl.ds(row, parts, stride=ref.shape[0] // parts), :]


def put_tiles(ref, tiles, first):
    for k in range(len(tiles[0]) - 1):
        for chan in range(OWN):
            put(ref, first + k * OWN + chan, tiles[chan][k])
    for pair in range(OWN // 2):
        halves = [tiles[2 * pair + k][-1] for k in range(2)]
        row = first + (len(tiles[0]) - 1) * OWN + pair
        put(ref, row, jnp.concatenate(halves, axis=1))


def take_tiles(ref, first, chan, parts):
    tiles = [take(ref, first + k * OWN + chan, parts) for k in range(4)]
    last = take(ref, first + 4 * OWN + chan // 2, parts)
    start = chan % 2 * (LANES // 2)
    return tiles + [last[:, start : start + LANES // 2]]


def take_rows(ref, tiles, parts):
    mine = [take_tiles(ref, 0, chan, parts) for chan in range(OWN)]
    return [jnp.concatenate([m[k] for m in mine], axis=0) for k in tiles]


def put_edges(both, proj):
    hidden = proj[0].shape[0] // 2
    parts = hidden // OWN
    for side, p in enumerate(proj):
        edge = sigmoid(p[:hidden]) * p[hidden:]
        tiles = [lane_tiles(edge[k : k + parts]) for k in range(0, hidden, parts)]
        put_tiles(both, tiles, side * 18)


def first_kernel(
    pair,
    norm_in,
    w_proj,
    w_gate,
    norm_mid,
    w_out,
    both,
    normed,
    state,
    norm_in_near,
    w_proj_near,
    w_gate_near,
    norm_mid_near,
    w_out_near,
    pair_near,
    sems,
):
    cols, chans = pair.shape[1:]
    half = cols // 2
    parts = cols // (ROWS * CORES)
    ends = [(norm_in, norm_in_near)]
    for k in range(ROWS):
        for h in (0, half):
            ends.append((pair.at[k, pl.ds(h, half)], pair_near.at[k, pl.ds(h, half)]))
    ends += [
        (w_proj.at[0], w_proj_near.at[0]),
        (w_gate, w_gate_near),
        (w_proj.at[1], w_proj_near.at[1]),
        (norm_mid, norm_mid_near),
        (w_out, w_out_near),
    ]
    moves = [pltpu.make_async_copy(*pair_of, sems.at[k]) for k, pair_of in enumerate(ends)]
    for move in moves:
        move.start()
    for move in moves[:7]:
        move.wait()
    value = jnp.transpose(
        jnp.concatenate(
            [
                pair_near[k, pl.ds(core * ROWS + j, parts, stride=CORES * ROWS), :]
                for k, j in blocks()
                for core in range(CORES)
            ],
            axis=0,
        )
    )
    state[...] = value
    gain = wide(norm_in_near[0:1, :])
    moves[7].wait()
    ready = norm_rows(value, gain)
    normed[...] = ready
    proj = mix(w_proj_near[0], ready)
    put_edges(both, (proj[: 2 * chans], proj[2 * chans :]))
    for move in moves[8:]:
        move.wait()


def middle_kernel(got, state, gate, w_proj, gains, units, w_out, both, normed, state_next):
    chans, places = state.shape
    parts = chans // OWN
    tri = take_rows(got, range(5), parts)
    tri = jnp.concatenate(tri, axis=1) * spread(units[0], places)
    value = state[...] + gate[...] * mix(w_out[0], norm_rows(tri, gains[0]))
    state_next[...] = value
    ready = norm_rows(value, gains[2])
    normed[...] = ready
    each = w_proj.shape[2] // 2
    proj = mix(w_proj[1], ready)
    put_edges(both, (proj[:each], proj[each:]))


def last_kernel(got, state, gate, gains, units, w_out, out, near, sems):
    cols, chans = out.shape[1:]
    parts = cols // (ROWS * CORES)
    order = [(k, core * ROWS + j) for k, j in blocks() for core in range(CORES)]
    moves = []
    for tiles, rows in (((0, 1, 3), (0, 1)), ((2, 4), (2,))):
        mine = [n for n in range(len(order)) if n // (2 * CORES) in tiles]
        width = len(mine) * parts

        def lanes(ref):
            pieces = [ref[:, k * LANES : min((k + 1) * LANES, ref.shape[1])] for k in tiles]
            return jnp.concatenate(pieces, axis=1)

        tri = jnp.concatenate(take_rows(got, tiles, parts), axis=1) * spread(units[1], width)
        value = lanes(state) + lanes(gate) * mix(w_out[1], norm_rows(tri, gains[1]))
        turned = jnp.transpose(value)
        for place, n in enumerate(mine):
            row, slot = order[n]
            near[row, pl.ds(slot, parts, stride=CORES * ROWS), :] = turned[
                place * parts : (place + 1) * parts
            ]
        block = pl.ds(rows[0], len(rows))
        move = pltpu.make_async_copy(near.at[block], out.at[block], sems.at[len(moves)])
        move.start()
        moves.append(move)
    for move in moves:
        move.wait()


def square(tiles):
    half = LANES // 2
    tails = [tiles[3][:, :half], tiles[3][:, half:], tiles[4]]
    return [jnp.concatenate([main, end], axis=1) for main, end in zip(tiles[:3], tails)]


def stack(rows):
    return jnp.concatenate(rows, axis=0).astype(BF16)


def product_tiles(rows, scale):
    tails = [row[:, LANES:] for row in rows]
    tiles = [row[:, :LANES] * scale for row in rows]
    tiles.append(jnp.concatenate(tails[:2], axis=1) * scale)
    return tiles + [tails[2] * scale[:, : LANES // 2]]


def scale_of(scales, chan):
    parts = scales.shape[0] // OWN
    return scales[pl.ds(chan * parts + lax.axis_index("chip"), 1), :]


def largest(gain, w_proj, cols):
    hidden = w_proj.shape[1] // 4
    weighted = [gain * w_proj[:, k : k + hidden].astype(F32) for k in (hidden, 3 * hidden)]
    left, right = (jnp.sum(w * w, axis=0, keepdims=True) for w in weighted)
    return 1.02 * cols * hidden * jnp.sqrt(left * right) + 1e-20


def prepare_kernel(
    got, normed, norm_in, w_proj, w_gate, norm_mid, left, own, gate, gains, units, scales
):
    parts = scales.shape[1] // OWN
    for which in range(2):
        gain = wide(norm_in[which : which + 1, :])
        bound = largest(gain, w_proj[which], parts * CORES * ROWS)
        scales[which] = wide(TOP / bound)
        units[which] = wide(bound * (1 / TOP))
        gains[which] = wide(norm_mid[which : which + 1, :])
    gains[2] = gain
    for chan in range(OWN):
        left[chan] = stack(square(take_tiles(got, 0, chan, parts)))
        own[chan] = stack(square(take_tiles(got, 18, chan, parts)))
    gate[...] = sigmoid(mix(w_gate[0], normed[...]))


def outgoing_kernel(left, own, other, scales, out):
    parts = scales.shape[1] // OWN
    first = lax.axis_index("core") == 0
    tiles = []
    for chan in range(OWN):
        far = stack(square(take_tiles(other, 0, chan, parts)))
        right = []
        for k in range(0, far.shape[0], parts):
            mine, theirs = own[chan, k : k + parts], far[k : k + parts]
            right += [jnp.where(first, mine, theirs), jnp.where(first, theirs, mine)]
        tri = lax.dot_general(
            left[chan],
            jnp.concatenate(right, axis=0),
            (((1,), (1,)), ((), ())),
            preferred_element_type=F32,
        )
        rows = [tri[k : k + parts] for k in range(0, tri.shape[0], parts)]
        tiles.append(product_tiles(rows, scale_of(scales.at[0], chan)))
    put_tiles(out, tiles, 0)


def half_sums(got, scales, out, core):
    parts = scales.shape[1] // OWN
    first = core == 0
    tiles, sums = [], []
    for chan in range(OWN):
        left = stack(square(take_tiles(got, 0, chan, parts)))
        right = stack(square(take_tiles(got, 18, chan, parts)))
        turned = jnp.transpose(left)
        rows = [turned[k : k + parts] for k in range(0, turned.shape[0], parts)]
        rows = [jnp.where(first, a, b) for a, b in zip(rows[0::2], rows[1::2])]
        sums.append(
            jnp.dot(jnp.concatenate(rows, axis=0), right, preferred_element_type=F32)
        )
    for chan, tri in enumerate(sums):
        rows = [tri[k : k + parts] for k in range(0, tri.shape[0], parts)]
        tiles.append(product_tiles(rows, scale_of(scales.at[1], chan)))
    put_tiles(out, tiles, 0)


def given_kernel(got, scales, out):
    half_sums(got, scales, out, 1 - lax.axis_index("core"))


def kept_kernel(got, scales, normed, w_gate, out, gate):
    half_sums(got, scales, out, lax.axis_index("core"))
    gate[...] = sigmoid(mix(w_gate[1], normed[...]))


def per_device(pair, norm_in, w_proj, w_gate, norm_mid, w_out):
    cols, chans = pair.shape[1:]
    parts = cols // (ROWS * CORES)
    places = ROWS * cols
    tri_t = jax.ShapeDtypeStruct((parts * OWN * places // LANES, LANES), F32)
    both_t = jax.ShapeDtypeStruct((2 * tri_t.shape[0], LANES), F32)
    flat_t = jax.ShapeDtypeStruct((chans, places), F32)
    normed_t = jax.ShapeDtypeStruct((chans, places), BF16)
    near = pl.BlockSpec(memory_space=pltpu.VMEM)
    far = pl.BlockSpec(memory_space=pl.ANY)
    dma = pltpu.SemaphoreType.DMA

    def call(kernel, ins, outs, scratch=(), in_spec=near, out_spec=near):
        return pl.pallas_call(
            kernel,
            in_specs=[in_spec] * len(ins),
            out_specs=[out_spec] * len(outs),
            out_shape=outs,
            scratch_shapes=scratch,
            compiler_params=pltpu.CompilerParams(vmem_limit_bytes=32 * 2**20),
        )(*ins)

    def exchange(value):
        sent = value.reshape(parts, -1, 2, LANES)
        return lax.all_to_all(sent, "chip", 0, 0, tiled=True)

    def swap(value):
        return lax.ppermute(value, "core", [(0, 1), (1, 0)])

    def rows_of(value):
        return value.reshape(-1, LANES).astype(F32)

    def like(array):
        return jax.ShapeDtypeStruct(array.shape, array.dtype)

    def squares(count):
        return jax.ShapeDtypeStruct((count, chans, chans), F32)

    params = (norm_in, w_proj, w_gate, norm_mid, w_out)
    both, normed, state, norm_in, w_proj, w_gate, norm_mid, w_out = call(
        first_kernel,
        tuple(pltpu.with_memory_space_constraint(a, pltpu.HBM) for a in (pair, *params)),
        [both_t, normed_t, flat_t, *map(like, params)],
        [pltpu.VMEM(pair.shape, F32), dma((12,))],
        in_spec=far,
    )
    got = exchange(both.astype(BF16))
    other = swap(got[:, got.shape[1] // 2 :])
    got = rows_of(got)
    square_t = jax.ShapeDtypeStruct((OWN, cols // CORES, cols), BF16)
    left, own, gate, gains, units, scales = call(
        prepare_kernel,
        (got, normed, norm_in, w_proj, w_gate, norm_mid),
        [square_t, square_t, flat_t, squares(3), squares(2), squares(2)],
    )
    (tri,) = call(outgoing_kernel, (left, own, rows_of(other), scales), [tri_t])
    got = exchange(tri.astype(jnp.float16))
    both, normed, state = call(
        middle_kernel,
        (rows_of(got), state, gate, w_proj, gains, units, w_out),
        [both_t, normed_t, flat_t],
    )
    got = rows_of(exchange(both.astype(BF16)))
    (given,) = call(given_kernel, (got, scales), [tri_t])
    other = swap(given.astype(jnp.float16))
    tri, gate = call(kept_kernel, (got, scales, normed, w_gate), [tri_t, flat_t])
    tri = tri + other.astype(F32)
    got = exchange(tri.astype(jnp.float16))
    (out,) = call(
        last_kernel,
        (rows_of(got), state, gate, gains, units, w_out),
        [like(pair)],
        [pltpu.VMEM(pair.shape, F32), dma((2,))],
        out_spec=far,
    )
    return out


def solution(mesh):
    crops, devices = mesh.devices.shape
    split = Mesh(mesh.devices.reshape(crops, devices // CORES, CORES), ("crop", "chip", "core"))
    whole = P(("crop", "chip", "core"), None, None)
    return jax.shard_map(
        per_device,
        mesh=split,
        in_specs=(whole, P(), P(), P(), P(), P()),
        out_specs=whole,
        check_vma=False,
    )
```

```python
import jax
import jax.numpy as jnp
from jax import lax
from jax.experimental import pallas as pl
from jax.experimental.pallas import tpu as pltpu
from jax.sharding import Mesh
from jax.sharding import PartitionSpec as P

F32 = jnp.float32
BF16 = jnp.bfloat16
LANES = 128
ROWS = 3
OWN = 4
CORES = 2
TOP = 2.0**14


def blocks():
    return [(k, j) for k in range(ROWS) for j in range(ROWS - 1)] + [
        (k, ROWS - 1) for k in range(ROWS)
    ]


def wide(row):
    return jnp.transpose(jnp.broadcast_to(row, (row.shape[1], row.shape[1])))


def spread(tile, width):
    whole = [tile] * (width // LANES)
    rest = [tile[:, : width % LANES]] if width % LANES else []
    return jnp.concatenate(whole + rest, axis=1)


def norm_rows(value, gain):
    mean = jnp.mean(value, axis=0, keepdims=True)
    cent = value - mean
    var = jnp.mean(cent * cent, axis=0, keepdims=True)
    return (cent * lax.rsqrt(var + 1e-05) * spread(gain, value.shape[1])).astype(BF16)


def mix(weight, value):
    return lax.dot_general(weight, value, (((0,), (0,)), ((), ())), preferred_element_type=F32)


def sigmoid(half):
    return 0.5 * jnp.tanh(half) + 0.5


def lane_tiles(value):
    return [value[:, k : k + LANES] for k in range(0, value.shape[1], LANES)]


def put(ref, row, value):
    ref[pl.ds(row, value.shape[0], stride=ref.shape[0] // value.shape[0]), :] = value


def take(ref, row, parts):
    return ref[pl.ds(row, parts, stride=ref.shape[0] // parts), :]


def put_tiles(ref, tiles, first):
    for k in range(len(tiles[0]) - 1):
        for chan in range(OWN):
            put(ref, first + k * OWN + chan, tiles[chan][k])
    for pair in range(OWN // 2):
        halves = [tiles[2 * pair + k][-1] for k in range(2)]
        row = first + (len(tiles[0]) - 1) * OWN + pair
        put(ref, row, jnp.concatenate(halves, axis=1))


def take_tiles(ref, first, chan, parts):
    tiles = [take(ref, first + k * OWN + chan, parts) for k in range(4)]
    last = take(ref, first + 4 * OWN + chan // 2, parts)
    start = chan % 2 * (LANES // 2)
    return tiles + [last[:, start : start + LANES // 2]]


def take_rows(ref, tiles, parts):
    mine = [take_tiles(ref, 0, chan, parts) for chan in range(OWN)]
    return [jnp.concatenate([m[k] for m in mine], axis=0) for k in tiles]


def put_edges(both, proj):
    hidden = proj[0].shape[0] // 2
    parts = hidden // OWN
    for side, p in enumerate(proj):
        edge = (jnp.tanh(p[:hidden]) + 1.0) * p[hidden:]
        tiles = [lane_tiles(edge[k : k + parts]) for k in range(0, hidden, parts)]
        put_tiles(both, tiles, side * 18)


def first_kernel(
    pair,
    norm_in,
    w_proj,
    w_gate,
    norm_mid,
    w_out,
    both,
    normed,
    state,
    norm_in_near,
    w_proj_near,
    w_gate_near,
    norm_mid_near,
    w_out_near,
    pair_near,
    sems,
):
    cols, chans = pair.shape[1:]
    half = cols // 2
    parts = cols // (ROWS * CORES)
    ends = [(norm_in, norm_in_near)]
    for k in range(ROWS):
        for h in (0, half):
            ends.append((pair.at[k, pl.ds(h, half)], pair_near.at[k, pl.ds(h, half)]))
    ends += [
        (w_proj.at[0], w_proj_near.at[0]),
        (w_gate, w_gate_near),
        (w_proj.at[1], w_proj_near.at[1]),
        (norm_mid, norm_mid_near),
        (w_out, w_out_near),
    ]
    moves = [pltpu.make_async_copy(*pair_of, sems.at[k]) for k, pair_of in enumerate(ends)]
    for move in moves:
        move.start()
    for move in moves[:7]:
        move.wait()
    value = jnp.transpose(
        jnp.concatenate(
            [
                pair_near[k, pl.ds(core * ROWS + j, parts, stride=CORES * ROWS), :]
                for k, j in blocks()
                for core in range(CORES)
            ],
            axis=0,
        )
    )
    state[...] = value
    gain = wide(0.5 * norm_in_near[0:1, :])
    moves[7].wait()
    ready = norm_rows(value, gain)
    normed[...] = ready
    proj = mix(w_proj_near[0], ready)
    put_edges(both, (proj[: 2 * chans], proj[2 * chans :]))
    for move in moves[8:]:
        move.wait()


def middle_kernel(got, state, gate, w_proj, gains, units, w_out, both, normed, state_next):
    chans, places = state.shape
    parts = chans // OWN
    tri = take_rows(got, range(5), parts)
    tri = jnp.concatenate(tri, axis=1) * spread(units[0], places)
    value = state[...] + gate[...] * mix(w_out[0], norm_rows(tri, gains[0]))
    state_next[...] = value
    ready = norm_rows(value, gains[2])
    normed[...] = ready
    each = w_proj.shape[2] // 2
    proj = mix(w_proj[1], ready)
    put_edges(both, (proj[:each], proj[each:]))


def last_kernel(got, state, gate, gains, units, w_out, out, near, sems):
    cols, chans = out.shape[1:]
    parts = cols // (ROWS * CORES)
    order = [(k, core * ROWS + j) for k, j in blocks() for core in range(CORES)]
    moves = []
    for tiles, rows in (((0, 1, 3), (0, 1)), ((2, 4), (2,))):
        mine = [n for n in range(len(order)) if n // (2 * CORES) in tiles]
        width = len(mine) * parts

        def lanes(ref):
            pieces = [ref[:, k * LANES : min((k + 1) * LANES, ref.shape[1])] for k in tiles]
            return jnp.concatenate(pieces, axis=1)

        tri = jnp.concatenate(take_rows(got, tiles, parts), axis=1) * spread(units[1], width)
        value = lanes(state) + lanes(gate) * mix(w_out[1], norm_rows(tri, gains[1]))
        turned = jnp.transpose(value)
        for place, n in enumerate(mine):
            row, slot = order[n]
            near[row, pl.ds(slot, parts, stride=CORES * ROWS), :] = turned[
                place * parts : (place + 1) * parts
            ]
        block = pl.ds(rows[0], len(rows))
        move = pltpu.make_async_copy(near.at[block], out.at[block], sems.at[len(moves)])
        move.start()
        moves.append(move)
    for move in moves:
        move.wait()


def square(tiles):
    half = LANES // 2
    tails = [tiles[3][:, :half], tiles[3][:, half:], tiles[4]]
    return [jnp.concatenate([main, end], axis=1) for main, end in zip(tiles[:3], tails)]


def stack(rows):
    return jnp.concatenate(rows, axis=0).astype(BF16)


def product_tiles(rows, scale):
    tails = [row[:, LANES:] for row in rows]
    tiles = [row[:, :LANES] * scale for row in rows]
    tiles.append(jnp.concatenate(tails[:2], axis=1) * scale)
    return tiles + [tails[2] * scale[:, : LANES // 2]]


def scale_of(scales, chan):
    parts = scales.shape[0] // OWN
    return scales[pl.ds(chan * parts + lax.axis_index("chip"), 1), :]


def largest(gain, w_proj, cols):
    hidden = w_proj.shape[1] // 4
    weighted = [gain * w_proj[:, k : k + hidden].astype(F32) for k in (hidden, 3 * hidden)]
    left, right = (jnp.sum(w * w, axis=0, keepdims=True) for w in weighted)
    return 1.02 * cols * hidden * jnp.sqrt(left * right) + 1e-20


def prepare_kernel(
    got, normed, norm_in, w_proj, w_gate, norm_mid, left, own, gate, gains, units, scales
):
    parts = scales.shape[1] // OWN
    for which in range(2):
        gain = wide(norm_in[which : which + 1, :])
        bound = largest(gain, w_proj[which], parts * CORES * ROWS)
        scales[which] = wide(TOP / bound)
        units[which] = wide(bound * (1 / TOP))
        gains[which] = wide(norm_mid[which : which + 1, :])
    gains[2] = 0.5 * gain
    for chan in range(OWN):
        left[chan] = stack(square(take_tiles(got, 0, chan, parts)))
        own[chan] = stack(square(take_tiles(got, 18, chan, parts)))
    gate[...] = sigmoid(mix(w_gate[0], normed[...]))


def outgoing_kernel(left, own, other, scales, out):
    parts = scales.shape[1] // OWN
    first = lax.axis_index("core") == 0
    tiles = []
    for chan in range(OWN):
        far = stack(square(take_tiles(other, 0, chan, parts)))
        right = []
        for k in range(0, far.shape[0], parts):
            mine, theirs = own[chan, k : k + parts], far[k : k + parts]
            right += [jnp.where(first, mine, theirs), jnp.where(first, theirs, mine)]
        tri = lax.dot_general(
            left[chan],
            jnp.concatenate(right, axis=0),
            (((1,), (1,)), ((), ())),
            preferred_element_type=F32,
        )
        rows = [tri[k : k + parts] for k in range(0, tri.shape[0], parts)]
        tiles.append(product_tiles(rows, scale_of(scales.at[0], chan)))
    put_tiles(out, tiles, 0)


def half_sums(got, scales, out, core):
    parts = scales.shape[1] // OWN
    first = core == 0
    tiles, sums = [], []
    for chan in range(OWN):
        left = stack(square(take_tiles(got, 0, chan, parts)))
        right = stack(square(take_tiles(got, 18, chan, parts)))
        turned = jnp.transpose(left)
        rows = [turned[k : k + parts] for k in range(0, turned.shape[0], parts)]
        rows = [jnp.where(first, a, b) for a, b in zip(rows[0::2], rows[1::2])]
        sums.append(
            jnp.dot(jnp.concatenate(rows, axis=0), right, preferred_element_type=F32)
        )
    for chan, tri in enumerate(sums):
        rows = [tri[k : k + parts] for k in range(0, tri.shape[0], parts)]
        tiles.append(product_tiles(rows, scale_of(scales.at[1], chan)))
    put_tiles(out, tiles, 0)


def given_kernel(got, scales, out):
    half_sums(got, scales, out, 1 - lax.axis_index("core"))


def kept_kernel(got, scales, normed, w_gate, out, gate):
    half_sums(got, scales, out, lax.axis_index("core"))
    gate[...] = sigmoid(mix(w_gate[1], normed[...]))


def per_device(pair, norm_in, w_proj, w_gate, norm_mid, w_out):
    cols, chans = pair.shape[1:]
    parts = cols // (ROWS * CORES)
    places = ROWS * cols
    tri_t = jax.ShapeDtypeStruct((parts * OWN * places // LANES, LANES), F32)
    both_t = jax.ShapeDtypeStruct((2 * tri_t.shape[0], LANES), F32)
    flat_t = jax.ShapeDtypeStruct((chans, places), F32)
    normed_t = jax.ShapeDtypeStruct((chans, places), BF16)
    near = pl.BlockSpec(memory_space=pltpu.VMEM)
    far = pl.BlockSpec(memory_space=pl.ANY)
    dma = pltpu.SemaphoreType.DMA

    def call(kernel, ins, outs, scratch=(), in_spec=near, out_spec=near):
        return pl.pallas_call(
            kernel,
            in_specs=[in_spec] * len(ins),
            out_specs=[out_spec] * len(outs),
            out_shape=outs,
            scratch_shapes=scratch,
            compiler_params=pltpu.CompilerParams(vmem_limit_bytes=32 * 2**20),
        )(*ins)

    def exchange(value):
        sent = value.reshape(parts, -1, 2, LANES)
        return lax.all_to_all(sent, "chip", 0, 0, tiled=True)

    def swap(value):
        return lax.ppermute(value, "core", [(0, 1), (1, 0)])

    def rows_of(value):
        return value.reshape(-1, LANES).astype(F32)

    def like(array):
        return jax.ShapeDtypeStruct(array.shape, array.dtype)

    def squares(count):
        return jax.ShapeDtypeStruct((count, chans, chans), F32)

    params = (norm_in, w_proj, w_gate, norm_mid, w_out)
    both, normed, state, norm_in, w_proj, w_gate, norm_mid, w_out = call(
        first_kernel,
        tuple(pltpu.with_memory_space_constraint(a, pltpu.HBM) for a in (pair, *params)),
        [both_t, normed_t, flat_t, *map(like, params)],
        [pltpu.VMEM(pair.shape, F32), dma((12,))],
        in_spec=far,
    )
    got = exchange(both.astype(BF16))
    other = swap(got[:, got.shape[1] // 2 :])
    got = rows_of(got)
    square_t = jax.ShapeDtypeStruct((OWN, cols // CORES, cols), BF16)
    left, own, gate, gains, units, scales = call(
        prepare_kernel,
        (got, normed, norm_in, w_proj, w_gate, norm_mid),
        [square_t, square_t, flat_t, squares(3), squares(2), squares(2)],
    )
    (tri,) = call(outgoing_kernel, (left, own, rows_of(other), scales), [tri_t])
    got = exchange(tri.astype(jnp.float16))
    both, normed, state = call(
        middle_kernel,
        (rows_of(got), state, gate, w_proj, gains, units, w_out),
        [both_t, normed_t, flat_t],
    )
    got = rows_of(exchange(both.astype(BF16)))
    (given,) = call(given_kernel, (got, scales), [tri_t])
    other = swap(given.astype(jnp.float16))
    tri, gate = call(kept_kernel, (got, scales, normed, w_gate), [tri_t, flat_t])
    tri = tri + other.astype(F32)
    got = exchange(tri.astype(jnp.float16))
    (out,) = call(
        last_kernel,
        (rows_of(got), state, gate, gains, units, w_out),
        [like(pair)],
        [pltpu.VMEM(pair.shape, F32), dma((2,))],
        out_spec=far,
    )
    return out


def solution(mesh):
    crops, devices = mesh.devices.shape
    split = Mesh(mesh.devices.reshape(crops, devices // CORES, CORES), ("crop", "chip", "core"))
    whole = P(("crop", "chip", "core"), None, None)
    return jax.shard_map(
        per_device,
        mesh=split,
        in_specs=(whole, P(), P(), P(), P(), P()),
        out_specs=whole,
        check_vma=False,
    )
```
